32 devices in a mesh: seq: 8 (over z, y), kv: 4 (over x, core).
Axes of the slice: x: 2, y: 2, z: 4, core: 2. Of those that a mesh axis runs over, the one named last changes fastest.
Arguments:
- queries: bfloat16 [2048, 28, 128], P('seq', 'kv'), may hold values from -8 to 8
- keys: bfloat16 [2048, 4, 128], P('seq', 'kv'), may hold values from -8 to 8
- values: bfloat16 [2048, 4, 128], P('seq', 'kv'), may hold values from -6 to 6
- out_weight: bfloat16 [3584, 3584], P('kv'), may hold values from -0.5 to 0.5
Outputs:
- layer_output: bfloat16 [2048, 3584], P('seq', 'kv')
The draws below stay inside these ranges and needn't reach their ends.
All inputs are finite; a program needn't handle non-finite values.
Results may differ from the reference program's by a relative error of at most 0.012.
Values may be sent and summed in bfloat16 or wider, within the bound.
No kernel may reach another device: no remote copies, remote signals or barrier semaphores. Data moves between devices by JAX's collectives and lax.ppermute only.
A program may use at most 64 MiB of HBM per device.

```python
import math
import jax
import jax.numpy as jnp
from jax import lax

HEAD = 128
GROUP = 7
H_KV = 4
HQ = 28
D = 3584
TOK_DEV = 256
SPAN = 1024
LOCAL = 32
TOKENS = 2048


def draw_queries(key, part):
    key = jax.random.fold_in(key, 11)
    drawn = jnp.clip(jax.random.normal(key, (TOKENS, HQ, HEAD), jnp.float32), -6.0, 6.0)
    return drawn.astype(jnp.bfloat16)


def draw_keys(key, part):
    key = jax.random.fold_in(key, 13)
    drawn = jnp.clip(jax.random.normal(key, (TOKENS, H_KV, HEAD), jnp.float32), -6.0, 6.0)
    return drawn.astype(jnp.bfloat16)


def block_scale(stream_key, shape, cuts, low, top_value):
    factor_of, own = 1.0, jax.random.fold_in(stream_key, 6)
    for axis_at, parts in cuts:
        heights = jnp.exp(jax.random.uniform(jax.random.fold_in(own, axis_at), (parts,), jnp.float32, low / len(cuts), top_value / len(cuts)))
        factor_of = factor_of * jnp.repeat(heights, shape[axis_at] // parts).reshape([-1 if axis == axis_at else 1 for axis in range(len(shape))])
    return factor_of


def centred(stream_key, extent, deviation, limit, shards=(), held_as=jnp.bfloat16):
    level = block_scale(stream_key, extent, shards, -0.22, 0.18) if shards else 1.0
    result = jax.random.normal(stream_key, extent, jnp.float32) * deviation * level
    return jnp.minimum(jnp.maximum(result, -limit), limit).astype(held_as)


def setup_inputs(seed: int = 0) -> dict:
    arg_keys = jax.random.split(jax.random.key(seed), 5)
    return {
        "queries": draw_queries(jax.random.fold_in(arg_keys[4], 71), 0),
        "keys": draw_keys(jax.random.fold_in(arg_keys[4], 71), 0),
        "values": centred(arg_keys[2], (TOKENS, H_KV, HEAD), 1.0, 6.0, ((0, 8), (1, 4))),
        "out_weight": centred(arg_keys[3], (D, D), HEAD ** -0.5, 0.5, ((0, 4),)),
    }


THETA = 10000000.0
NEG = -1e+30

def rotate(block_data, position):
    half_width = block_data.shape[-1] // 2
    ladder = jnp.arange(half_width, dtype=jnp.float32)
    inverse = jnp.exp(ladder * (-2.0 * math.log(THETA) / block_data.shape[-1]))
    angles = position.astype(jnp.float32)[..., None] * inverse
    cosine = jnp.cos(angles)
    sine_part = jnp.sin(angles)
    widened = block_data.astype(jnp.float32)
    first_half = widened[..., :half_width]
    second = widened[..., half_width:]
    return jnp.concatenate([first_half * cosine - second * sine_part, second * cosine + first_half * sine_part], axis=-1).astype(jnp.bfloat16)

def reference(queries, keys, values, out_weight):
    token_ids = jnp.arange(TOKENS, dtype=jnp.int32)
    key_rot = rotate(keys, jnp.broadcast_to((token_ids % SPAN)[:, None], (TOKENS, H_KV)))
    score_scale = 1.0 / math.sqrt(HEAD)
    block_rows = min(TOK_DEV, SPAN)
    zero_index = jnp.zeros((), jnp.int32)
    pad_keys = jnp.concatenate([jnp.zeros((SPAN, H_KV, HEAD), jnp.bfloat16), key_rot], 0)
    pad_values = jnp.concatenate([jnp.zeros((SPAN, H_KV, HEAD), jnp.bfloat16), values], 0)
    key_spans = token_ids // SPAN

    def per_block(block_index):
        first_row = (block_index * block_rows).astype(jnp.int32)
        span_index = first_row // SPAN
        tokens = first_row + jnp.arange(block_rows, dtype=jnp.int32)
        offset = tokens % SPAN
        row_tokens = jnp.repeat(tokens, GROUP)

        def spread(position):
            return jnp.broadcast_to(position[:, None], (block_rows, GROUP))

        def per_head(head_index):
            query_block = lax.dynamic_slice(queries, (first_row, (head_index * GROUP).astype(jnp.int32), zero_index), (block_rows, GROUP, HEAD))
            inner_query = rotate(query_block, spread(offset)).reshape(block_rows * GROUP, HEAD)
            adjacent_query = rotate(query_block, spread(jnp.minimum(offset + SPAN, SPAN + LOCAL))).reshape(block_rows * GROUP, HEAD)
            distant_query = rotate(query_block, spread(jnp.full_like(offset, SPAN + LOCAL))).reshape(block_rows * GROUP, HEAD)
            head_keys = lax.dynamic_index_in_dim(key_rot, head_index, 1, keepdims=False)
            head_values = lax.dynamic_index_in_dim(values, head_index, 1, keepdims=False)
            near_keys = lax.dynamic_slice(lax.dynamic_index_in_dim(pad_keys, head_index, 1, keepdims=False), ((span_index * SPAN).astype(jnp.int32), zero_index), (2 * SPAN, HEAD))
            near_values = lax.dynamic_slice(lax.dynamic_index_in_dim(pad_values, head_index, 1, keepdims=False), ((span_index * SPAN).astype(jnp.int32), zero_index), (2 * SPAN, HEAD))
            distant_scores = jnp.dot(distant_query, head_keys.T, preferred_element_type=jnp.float32) * score_scale
            adjacent_scores = jnp.dot(adjacent_query, near_keys[:SPAN].T, preferred_element_type=jnp.float32) * score_scale
            inner_scores = jnp.dot(inner_query, near_keys[SPAN:].T, preferred_element_type=jnp.float32) * score_scale
            distant_mask = jnp.broadcast_to((key_spans < span_index - 1)[None, :], distant_scores.shape)
            adjacent_mask = jnp.broadcast_to(span_index >= 1, adjacent_scores.shape)
            inner_tokens = span_index * SPAN + jnp.arange(SPAN, dtype=jnp.int32)
            inner_mask = inner_tokens[None, :] <= row_tokens[:, None]
            distant_masked = jnp.where(distant_mask, distant_scores, NEG)
            adjacent_masked = jnp.where(adjacent_mask, adjacent_scores, NEG)
            inner_masked = jnp.where(inner_mask, inner_scores, NEG)
            row_max = jnp.maximum(jnp.maximum(lax.optimization_barrier(jnp.max(distant_masked, axis=1)), lax.optimization_barrier(jnp.max(adjacent_masked, axis=1))), lax.optimization_barrier(jnp.max(inner_masked, axis=1)))
            distant_weights = jnp.where(distant_mask, jnp.exp(distant_masked - row_max[:, None]), 0.0)
            adjacent_weights = jnp.where(adjacent_mask, jnp.exp(adjacent_masked - row_max[:, None]), 0.0)
            inner_weights = jnp.where(inner_mask, jnp.exp(inner_masked - row_max[:, None]), 0.0)
            denominator = lax.optimization_barrier(jnp.sum(distant_weights, axis=1)) + lax.optimization_barrier(jnp.sum(adjacent_weights, axis=1)) + lax.optimization_barrier(jnp.sum(inner_weights, axis=1))
            numerator = jnp.dot(distant_weights.astype(jnp.bfloat16), head_values, preferred_element_type=jnp.float32)
            numerator = numerator + jnp.dot(adjacent_weights.astype(jnp.bfloat16), near_values[:SPAN], preferred_element_type=jnp.float32)
            numerator = numerator + jnp.dot(inner_weights.astype(jnp.bfloat16), near_values[SPAN:], preferred_element_type=jnp.float32)
            attended = (numerator / denominator[:, None]).astype(jnp.bfloat16)
            return attended.reshape(block_rows, GROUP, HEAD)
        return lax.map(per_head, jnp.arange(H_KV, dtype=jnp.int32))
    stacked = lax.map(per_block, jnp.arange(TOKENS // block_rows, dtype=jnp.int32))
    attended = jnp.transpose(stacked, (0, 2, 1, 3, 4)).reshape(TOKENS, HQ * HEAD)
    return jnp.dot(attended, out_weight, preferred_element_type=jnp.float32).astype(jnp.bfloat16)
```

```python
import functools
import math

import jax
import jax.numpy as jnp
import numpy as np
from jax import lax
from jax.experimental import pallas as pl
from jax.experimental.pallas import tpu as pltpu
from jax.sharding import PartitionSpec as P

HEAD = 128
GROUP = 7
SPAN = 1024
LOCAL = 32
THETA = 10000000.0
NEG = -1e30
SCALE = math.log2(math.e) / math.sqrt(HEAD)
ROW_CHUNKS = 2
VMEM = pltpu.MemorySpace.VMEM


def rope_tables(block):
    inverse = np.exp(np.arange(HEAD // 2, dtype=np.float64) * (-2.0 * math.log(THETA) / HEAD))
    inner = np.arange(SPAN)
    first = np.minimum(np.arange(block) + SPAN, SPAN + LOCAL)
    far = np.full((block,), SPAN + LOCAL)
    angles = np.concatenate([inner, first, far])[:, None] * inverse
    cosine, sine = np.cos(angles), np.sin(angles)
    return (
        jnp.asarray(np.concatenate([cosine, cosine], 1), jnp.float32),
        jnp.asarray(np.concatenate([-sine, sine], 1), jnp.float32),
    )


def rotated(x, cosine, sine):
    x = x.astype(jnp.float32)
    return x * cosine + pltpu.roll(x, HEAD // 2, 1) * sine


def prepare_kernel(rank, key_ref, value_ref, cos_ref, sin_ref, out_ref):
    block = key_ref.shape[0]
    out_ref[:block] = rotated(key_ref[...], cos_ref[...], sin_ref[...]).astype(jnp.bfloat16)
    out_ref[block:] = value_ref[...]


def prepare(rank, keys, values, tables):
    block = keys.shape[0]
    per_span = SPAN // block
    table = pl.BlockSpec((block, HEAD), lambda i, rank: (rank[0] % per_span, 0))
    whole = pl.BlockSpec((block, HEAD), lambda i, rank: (0, 0))
    return pl.pallas_call(
        prepare_kernel,
        grid_spec=pltpu.PrefetchScalarGridSpec(
            num_scalar_prefetch=1,
            grid=(1,),
            in_specs=[whole, whole, table, table],
            out_specs=pl.BlockSpec((2 * block, HEAD), lambda i, rank: (0, 0)),
        ),
        out_shape=jax.ShapeDtypeStruct((2 * block, HEAD), jnp.bfloat16),
        name="rotate_keys",
    )(rank, keys, values, *tables)


def attend_kernel(offsets, groups, first, last, block, row_chunk, *refs):
    rank = refs[0][0]
    refs = list(refs[1:])
    query_ref = refs.pop(0)
    table_refs = {group: (refs.pop(0), refs.pop(0)) for group in groups}
    piece_refs = [refs.pop(0) for _ in offsets]
    if not first:
        old_acc, old_stats = refs.pop(0), refs.pop(0)
    rows = query_ref.shape[1]
    per_span = SPAN // block
    owners = [rank ^ offset for offset in offsets]
    lifts = [
        None if offset == 0 else jnp.where(owner <= rank, 0.0, -NEG).astype(jnp.float32)
        for offset, owner in zip(offsets, owners)
    ]
    tables = {group: (c[...], s[...]) for group, (c, s) in table_refs.items()}
    if 0 in offsets:
        causal = lax.broadcasted_iota(jnp.int32, (rows, block), 1) <= lax.broadcasted_iota(
            jnp.int32, (rows, block), 0
        ) + row_chunk * rows
    for head in range(GROUP):
        query = query_ref[head]
        by_group = {
            group: (rotated(query, c, s) * SCALE).astype(jnp.bfloat16)
            for group, (c, s) in tables.items()
        }
        scores = []
        for offset, piece in zip(offsets, piece_refs):
            score = lax.dot_general(
                by_group[offset // per_span],
                piece[:block],
                (((1,), (1,)), ((), ())),
                preferred_element_type=jnp.float32,
            )
            if offset == 0:
                score = jnp.where(causal, score, NEG)
            scores.append(score)
        tops = [jnp.max(score, axis=1, keepdims=True) for score in scores]
        tops = [top if lift is None else top - lift for top, lift in zip(tops, lifts)]
        top = functools.reduce(jnp.maximum, tops)
        if first:
            total = jnp.zeros_like(top)
            acc = jnp.zeros((rows, HEAD), jnp.float32)
        else:
            old_top = old_stats[:, head : head + 1]
            top = jnp.maximum(top, old_top)
            factor = jnp.exp2(old_top - top)
            total = factor * old_stats[:, GROUP + head : GROUP + head + 1]
            acc = factor * old_acc[head]
        for score, lift, piece in zip(scores, lifts, piece_refs):
            weight = jnp.exp2(score - (top if lift is None else top + lift))
            total = total + jnp.sum(weight, axis=1, keepdims=True)
            acc = acc + jnp.dot(
                weight.astype(jnp.bfloat16), piece[block:], preferred_element_type=jnp.float32
            )
        if last:
            (out_ref,) = refs
            out_ref[:, head * HEAD : (head + 1) * HEAD] = (acc / total).astype(jnp.bfloat16)
        else:
            new_acc, new_stats = refs
            new_acc[head] = acc
            new_stats[:, head : head + 1] = top
            new_stats[:, GROUP + head : GROUP + head + 1] = total


def attend(rank, offsets, queries, pieces, tables, state, last, row_chunk=0, row_chunks=1):
    block = pieces[0].shape[0] // 2
    rows = block // row_chunks
    per_span = SPAN // block
    groups = sorted({offset // per_span for offset in offsets})
    first = state is None

    def table_at(group):
        def index(i, rank):
            spans_back = rank[0] // per_span - (rank[0] ^ (group * per_span)) // per_span
            at_first = rank[0] % per_span == 0
            inner = rank[0] % per_span
            near = jnp.where(at_first, per_span, per_span + 1)
            place = jnp.where(spans_back == 1, near, per_span + 1)
            place = jnp.where(spans_back == 0, inner, place)
            return (place * row_chunks + row_chunk, 0)

        return pl.BlockSpec((rows, HEAD), index)

    by_head = pl.BlockSpec((GROUP, rows, HEAD), lambda i, rank: (0, row_chunk, 0))
    by_row = pl.BlockSpec((rows, HEAD), lambda i, rank: (row_chunk, 0))
    in_specs = [by_head]
    args = [queries]
    for group in groups:
        in_specs += [table_at(group)] * 2
        args += list(tables)
    in_specs += [pl.BlockSpec((2 * block, HEAD), lambda i, rank: (0, 0))] * len(pieces)
    args += pieces
    if not first:
        in_specs += [by_head, by_row]
        args += list(state)
    if last:
        out_specs = pl.BlockSpec((rows, GROUP * HEAD), lambda i, rank: (0, 0))
        out_shape = jax.ShapeDtypeStruct((rows, GROUP * HEAD), jnp.bfloat16)
    else:
        out_specs = [
            pl.BlockSpec((GROUP, rows, HEAD), lambda i, rank: (0, 0, 0)),
            pl.BlockSpec((rows, HEAD), lambda i, rank: (0, 0)),
        ]
        out_shape = [
            jax.ShapeDtypeStruct((GROUP, rows, HEAD), jnp.float32),
            jax.ShapeDtypeStruct((rows, HEAD), jnp.float32),
        ]
    kernel = functools.partial(
        attend_kernel, tuple(offsets), tuple(groups), first, last, block, row_chunk
    )
    pairs = GROUP * rows * block * len(pieces)
    return pl.pallas_call(
        kernel,
        grid_spec=pltpu.PrefetchScalarGridSpec(
            num_scalar_prefetch=1, grid=(1,), in_specs=in_specs, out_specs=out_specs
        ),
        out_shape=out_shape,
        cost_estimate=pl.CostEstimate(
            flops=4 * HEAD * pairs, bytes_accessed=2**21, transcendentals=pairs
        ),
        compiler_params=pltpu.CompilerParams(vmem_limit_bytes=24 * 2**20),
        name="attend_" + "_".join(map(str, offsets)),
    )(rank, *args)


def project_kernel(flip, place, own_ref, twin_ref, own_weight, twin_weight, out_ref):
    out_ref[...] = (
        jnp.dot(own_ref[...], own_weight[...], preferred_element_type=jnp.float32)
        + jnp.dot(twin_ref[...], twin_weight[...], preferred_element_type=jnp.float32)
    ).astype(out_ref.dtype)


def project(place, flip, own, twin, own_weight, twin_weight, dtype):
    rows, depth = own.shape
    kv_parts = own_weight.shape[1] // depth
    columns = own_weight.shape[1] // kv_parts
    whole = pl.BlockSpec((rows, depth), lambda i, place: (0, 0))
    weight = pl.BlockSpec((depth, columns), lambda i, place: (0, place[0] ^ flip))
    return pl.pallas_call(
        functools.partial(project_kernel, flip),
        grid_spec=pltpu.PrefetchScalarGridSpec(
            num_scalar_prefetch=1,
            grid=(1,),
            in_specs=[whole, whole, weight, weight],
            out_specs=pl.BlockSpec((rows, columns), lambda i, place: (0, 0)),
        ),
        out_shape=jax.ShapeDtypeStruct((rows, columns), dtype),
        cost_estimate=pl.CostEstimate(
            flops=4 * rows * depth * columns, bytes_accessed=4 * depth * columns, transcendentals=0
        ),
        compiler_params=pltpu.CompilerParams(vmem_limit_bytes=24 * 2**20),
        name="project_%d" % flip,
    )(place, own, twin, own_weight, twin_weight)


def swap(x, axis, size, bits):
    return lax.ppermute(x, axis, [(i, i ^ bits) for i in range(size)])


def make_shards(seq, kv):
    def shards(queries, keys, values, out_weight):
        block = queries.shape[0]
        per_span = SPAN // block
        rank = lax.axis_index("seq").astype(jnp.int32).reshape(1)
        place = lax.axis_index("kv").astype(jnp.int32).reshape(1)
        tables = rope_tables(block)
        by_head = jnp.transpose(queries, (1, 0, 2))
        twin_weight = swap(out_weight, "kv", kv, 1)
        pieces = {0: prepare(rank, keys[:, 0, :], values[:, 0, :], tables)}

        def fetch(offset):
            if offset not in pieces:
                low = offset % per_span
                step = low if low else offset & -offset
                pieces[offset] = swap(fetch(offset - step), "seq", seq, step)
            return pieces[offset]

        order = []
        step = per_span
        while step < seq:
            order.append(step)
            step *= 2
        for offset in order + list(range(1, min(per_span, seq))) + list(range(seq)):
            fetch(offset)
        calls = [[0, 1], [2, 3, 4]]
        while calls[-1][-1] < seq - 1:
            start = calls[-1][-1] + 1
            calls.append(list(range(start, min(start + per_span, seq))))
        state = None
        for offsets in calls[:-1]:
            state = attend(
                rank, offsets, by_head, [pieces[o] for o in offsets], tables, state, False
            )
        results = []
        for chunk in range(ROW_CHUNKS):
            offsets = calls[-1]
            own = attend(
                rank,
                offsets,
                by_head,
                [pieces[o] for o in offsets],
                tables,
                state,
                True,
                chunk,
                ROW_CHUNKS,
            )
            twin = swap(own, "kv", kv, 1)
            away = project(place, 2, own, twin, out_weight, twin_weight, jnp.bfloat16)
            landed = swap(away, "kv", kv, 2)
            home = project(place, 0, own, twin, out_weight, twin_weight, jnp.float32)
            results.append((home, landed))
        return jnp.concatenate(
            [(home + landed.astype(jnp.float32)).astype(jnp.bfloat16) for home, landed in results], 0
        )

    return shards


def solution(mesh):
    return jax.shard_map(
        make_shards(mesh.shape["seq"], mesh.shape["kv"]),
        mesh=mesh,
        in_specs=(P("seq", "kv", None), P("seq", "kv", None), P("seq", "kv", None), P("kv", None)),
        out_specs=P("seq", "kv"),
        check_vma=False,
    )
```

```python
import functools
import math

import jax
import jax.numpy as jnp
import numpy as np
from jax import lax
from jax.experimental import pallas as pl
from jax.experimental.pallas import tpu as pltpu
from jax.sharding import PartitionSpec as P

HEAD = 128
GROUP = 7
SPAN = 1024
LOCAL = 32
THETA = 10000000.0
NEG = -1e30
SCALE = math.log2(math.e) / math.sqrt(HEAD)
ROW_CHUNKS = 2
VMEM = pltpu.MemorySpace.VMEM
HBM = pltpu.MemorySpace.HBM
LIMIT = 24 * 2**20


def rope_tables(block):
    inverse = np.exp(np.arange(HEAD // 2, dtype=np.float64) * (-2.0 * math.log(THETA) / HEAD))
    inner = np.arange(SPAN)
    first = np.minimum(np.arange(block) + SPAN, SPAN + LOCAL)
    far = np.full((block,), SPAN + LOCAL)
    angles = np.concatenate([inner, first, far])[:, None] * inverse
    cosine, sine = np.cos(angles), np.sin(angles)
    return (
        jnp.asarray(np.concatenate([cosine, cosine], 1), jnp.float32),
        jnp.asarray(np.concatenate([-sine, sine], 1), jnp.float32),
    )


def rotated(x, cosine, sine):
    x = x.astype(jnp.float32)
    return x * cosine + pltpu.roll(x, HEAD // 2, 1) * sine


def in_hbm(x):
    return pltpu.with_memory_space_constraint(x, HBM)


def prepare_kernel(rank_ref, key_hbm, value_hbm, cos_hbm, sin_hbm, out_ref, key_ref, cos_ref, sin_ref, sems):
    block = key_ref.shape[0]
    rows = pl.ds(pl.multiple_of(rank_ref[0] % (SPAN // block) * block, block), block)
    copies = [
        pltpu.make_async_copy(key_hbm, key_ref, sems.at[0]),
        pltpu.make_async_copy(cos_hbm.at[rows], cos_ref, sems.at[1]),
        pltpu.make_async_copy(sin_hbm.at[rows], sin_ref, sems.at[2]),
        pltpu.make_async_copy(value_hbm, out_ref.at[pl.ds(block, block)], sems.at[3]),
    ]
    for copy in copies:
        copy.start()
    for copy in copies:
        copy.wait()
    out_ref[:block] = rotated(key_ref[...], cos_ref[...], sin_ref[...]).astype(jnp.bfloat16)


def prepare(rank, keys, values, tables):
    block = keys.shape[0]
    return pl.pallas_call(
        prepare_kernel,
        in_specs=[pl.BlockSpec(memory_space=pltpu.SMEM)] + [pl.BlockSpec(memory_space=HBM)] * 4,
        out_specs=pl.BlockSpec(memory_space=VMEM),
        out_shape=jax.ShapeDtypeStruct((2 * block, HEAD), jnp.bfloat16),
        scratch_shapes=[
            pltpu.VMEM((block, HEAD), jnp.bfloat16),
            pltpu.VMEM((block, HEAD), jnp.float32),
            pltpu.VMEM((block, HEAD), jnp.float32),
            pltpu.SemaphoreType.DMA((4,)),
        ],
        compiler_params=pltpu.CompilerParams(vmem_limit_bytes=LIMIT),
        name="rotate_keys",
    )(rank, *[in_hbm(x) for x in (keys, values, *tables)])


def scores_of(query, pieces):
    block = pieces[0].shape[0] // 2
    return [
        lax.dot_general(
            q, piece[:block], (((1,), (1,)), ((), ())), preferred_element_type=jnp.float32
        )
        for q, piece in zip(query, pieces)
    ]


def absorb(scores, lifts, pieces, old):
    block = pieces[0].shape[0] // 2
    lanes = [slice(at, at + HEAD) for at in range(0, block, HEAD)]
    peak = None
    for score, lift in zip(scores, lifts):
        high = functools.reduce(jnp.maximum, [score[:, lane] for lane in lanes])
        if lift is not None:
            high = high - lift
        peak = high if peak is None else jnp.maximum(peak, high)
    top = jnp.max(peak, axis=1, keepdims=True)
    if old is None:
        top = jnp.broadcast_to(top, peak.shape)
        acc, total = None, None
    else:
        top = jnp.maximum(top, old[0])
        factor = jnp.exp2(old[0] - top)
        acc, total = factor * old[1], factor * old[2]
    ones = jnp.ones((block, HEAD), jnp.bfloat16)
    for score, lift, piece in zip(scores, lifts, pieces):
        base = top if lift is None else top + lift
        weight = jnp.exp2(score - jnp.concatenate([base] * len(lanes), 1)).astype(jnp.bfloat16)
        both = jnp.dot(
            weight, jnp.concatenate([piece[block:], ones], 1), preferred_element_type=jnp.float32
        )
        acc = both[:, :HEAD] if acc is None else acc + both[:, :HEAD]
        total = both[:, HEAD:] if total is None else total + both[:, HEAD:]
    return top, acc, total


def begin_kernel(
    kinds, rank_ref, place_ref, query_hbm, cos_hbm, sin_hbm, weight_hbm, piece_ref,
    rot_ref, top_ref, acc_ref, total_ref, mine_ref, query_ref, cos_ref, sin_ref, sems, weight_sems,
):
    heads, block, _ = query_ref.shape
    per_span = SPAN // block
    rank, place = rank_ref[0], place_ref[0]
    inner = rank % per_span
    places = [inner, jnp.where(inner == 0, per_span, per_span + 1), per_span + 1][:kinds]
    copies = [pltpu.make_async_copy(query_hbm, query_ref, sems.at[0])]
    for kind, at in enumerate(places):
        rows = pl.ds(pl.multiple_of(at * block, block), block)
        copies.append(pltpu.make_async_copy(cos_hbm.at[rows], cos_ref.at[kind], sems.at[1 + 2 * kind]))
        copies.append(pltpu.make_async_copy(sin_hbm.at[rows], sin_ref.at[kind], sems.at[2 + 2 * kind]))
    for copy in copies:
        copy.start()
    loads = column_copies(place, weight_hbm, mine_ref, weight_sems)
    for copy in loads:
        copy.start()
    for copy in copies:
        copy.wait()
    causal = lax.broadcasted_iota(jnp.int32, (block, block), 1) <= lax.broadcasted_iota(
        jnp.int32, (block, block), 0
    )
    for head in range(heads):
        for kind in range(kinds):
            rot_ref[kind, head] = (
                rotated(query_ref[head], cos_ref[kind], sin_ref[kind]) * SCALE
            ).astype(jnp.bfloat16)
    later = scores_of([rot_ref[0, 0]], [piece_ref])
    for head in range(heads):
        now = later
        if head + 1 < heads:
            later = scores_of([rot_ref[0, head + 1]], [piece_ref])
        now = [jnp.where(causal, now[0], NEG)]
        top_ref[head], acc_ref[head], total_ref[head] = absorb(now, [None], [piece_ref], None)
    for copy in loads:
        copy.wait()


def begin(kinds, rank, place, queries, tables, out_weight, piece):
    heads, block, _ = queries.shape
    depth = out_weight.shape[0]
    smem, hbm, vmem = (pl.BlockSpec(memory_space=space) for space in (pltpu.SMEM, HBM, VMEM))
    halves = jax.ShapeDtypeStruct((2, depth, depth), jnp.bfloat16)
    return pl.pallas_call(
        functools.partial(begin_kernel, kinds),
        in_specs=[smem, smem, hbm, hbm, hbm, hbm, vmem],
        out_specs=[vmem] * 5,
        out_shape=[
            jax.ShapeDtypeStruct((kinds, heads, block, HEAD), jnp.bfloat16),
            *[jax.ShapeDtypeStruct((heads, block, HEAD), jnp.float32)] * 3,
            halves,
        ],
        scratch_shapes=[
            pltpu.VMEM((heads, block, HEAD), jnp.bfloat16),
            pltpu.VMEM((kinds, block, HEAD), jnp.float32),
            pltpu.VMEM((kinds, block, HEAD), jnp.float32),
            pltpu.SemaphoreType.DMA((1 + 2 * kinds,)),
            pltpu.SemaphoreType.DMA((2,)),
        ],
        cost_estimate=pl.CostEstimate(flops=2 * 10**9, bytes_accessed=2**23, transcendentals=10**6),
        compiler_params=pltpu.CompilerParams(vmem_limit_bytes=LIMIT),
        name="attend_0",
    )(rank, place, *[in_hbm(x) for x in (queries, *tables, out_weight)], piece)


def column_copies(place, weight_hbm, into, sems):
    columns = into.shape[2]
    copies = []
    for flip in range(2):
        at = pl.ds(pl.multiple_of((place ^ (2 * flip)) * columns, columns), columns)
        copies.append(pltpu.make_async_copy(weight_hbm.at[:, at], into.at[flip], sems.at[flip]))
    return copies


def attend_kernel(offsets, kinds, last, start, rows, stages, rank_ref, rot_ref, *refs):
    pieces, refs = refs[: len(offsets)], refs[len(offsets) :]
    old, refs = refs[:3], refs[3:]
    loads = []
    if stages:
        place_ref, weight_hbm, *refs, staged_ref, sems = refs
        loads = column_copies(place_ref[0], weight_hbm, staged_ref, sems)
    for copy in loads:
        copy.start()
    block = pieces[0].shape[0] // 2
    per_span = SPAN // block
    rank = rank_ref[0]
    lifts = [jnp.where((rank ^ offset) <= rank, 0.0, -NEG).astype(jnp.float32) for offset in offsets]
    picked = []
    for offset in offsets:
        kind = min(offset // per_span, 1)
        if kind and kinds > 2:
            back = rank // per_span - (rank ^ offset) // per_span
            kind = jnp.clip(back, 1, kinds - 1)
        picked.append(kind)
    here = slice(start, start + rows)
    def scores_at(head):
        return scores_of([rot_ref[kind, head, here] for kind in picked], pieces)

    later = scores_at(0)
    for head in range(GROUP):
        now = later
        if head + 1 < GROUP:
            later = scores_at(head + 1)
        top, acc, total = absorb(now, lifts, pieces, [ref[head, here] for ref in old])
        if last:
            (out_ref,) = refs
            out_ref[:, head * HEAD : (head + 1) * HEAD] = (acc / total).astype(jnp.bfloat16)
        else:
            refs[0][head], refs[1][head], refs[2][head] = top, acc, total
    for copy in loads:
        copy.wait()


def attend(rank, offsets, rot, pieces, state, last, start, rows, stage=()):
    block = pieces[0].shape[0] // 2
    smem, vmem = (pl.BlockSpec(memory_space=space) for space in (pltpu.SMEM, VMEM))
    if last:
        out_specs = vmem
        out_shape = jax.ShapeDtypeStruct((rows, GROUP * HEAD), jnp.bfloat16)
    else:
        out_specs = [vmem] * 3
        out_shape = [jax.ShapeDtypeStruct((GROUP, rows, HEAD), jnp.float32)] * 3
    args, in_specs, scratch = [], [], []
    if stage:
        place, weight = stage
        depth = weight.shape[0]
        args = [place, in_hbm(weight)]
        in_specs = [smem, pl.BlockSpec(memory_space=HBM)]
        out_specs = [*out_specs, vmem]
        out_shape = [*out_shape, jax.ShapeDtypeStruct((2, depth, depth), jnp.bfloat16)]
        scratch = [pltpu.SemaphoreType.DMA((2,))]
    pairs = GROUP * rows * block * len(pieces)
    return pl.pallas_call(
        functools.partial(
            attend_kernel, tuple(offsets), rot.shape[0], last, start, rows, bool(stage)
        ),
        in_specs=[smem] + [vmem] * (4 + len(pieces)) + in_specs,
        scratch_shapes=scratch,
        out_specs=out_specs,
        out_shape=out_shape,
        cost_estimate=pl.CostEstimate(
            flops=8 * HEAD * pairs, bytes_accessed=2**21, transcendentals=pairs
        ),
        compiler_params=pltpu.CompilerParams(vmem_limit_bytes=LIMIT),
        name="attend_" + "_".join(map(str, offsets)),
    )(rank, rot, *pieces, *state, *args)


def project_kernel(flip, own_ref, twin_ref, own_weight, twin_weight, out_ref):
    out_ref[...] = (
        jnp.dot(own_ref[...], own_weight[flip], preferred_element_type=jnp.float32)
        + jnp.dot(twin_ref[...], twin_weight[flip], preferred_element_type=jnp.float32)
    ).astype(out_ref.dtype)


def project(flip, own, twin, own_weight, twin_weight, dtype):
    rows, depth = own.shape
    columns = own_weight.shape[2]
    vmem = pl.BlockSpec(memory_space=VMEM)
    return pl.pallas_call(
        functools.partial(project_kernel, flip),
        in_specs=[vmem] * 4,
        out_specs=vmem,
        out_shape=jax.ShapeDtypeStruct((rows, columns), dtype),
        cost_estimate=pl.CostEstimate(
            flops=4 * rows * depth * columns, bytes_accessed=2 * depth * columns, transcendentals=0
        ),
        compiler_params=pltpu.CompilerParams(vmem_limit_bytes=LIMIT),
        name="project_away" if flip else "project_home",
    )(own, twin, own_weight, twin_weight)


def close_kernel(starts, *refs):
    out_ref = refs[-1]
    for at, start in enumerate(starts):
        home, landed = refs[2 * at], refs[2 * at + 1]
        out_ref[start : start + home.shape[0]] = (
            home[...] + landed[...].astype(jnp.float32)
        ).astype(out_ref.dtype)


def close(parts):
    starts, rows = [], 0
    for home, _ in parts:
        starts.append(rows)
        rows += home.shape[0]
    vmem = pl.BlockSpec(memory_space=VMEM)
    return pl.pallas_call(
        functools.partial(close_kernel, tuple(starts)),
        in_specs=[vmem] * (2 * len(parts)),
        out_specs=vmem,
        out_shape=jax.ShapeDtypeStruct((rows, parts[0][0].shape[1]), jnp.bfloat16),
        compiler_params=pltpu.CompilerParams(vmem_limit_bytes=LIMIT),
        name="close",
    )(*[x for part in parts for x in part])


def swap(x, axis, size, bits):
    return lax.ppermute(x, axis, [(i, i ^ bits) for i in range(size)])


def after(x, *others):
    return lax.optimization_barrier((x, *others))[0]


def make_shards(seq, kv):
    def shards(queries, keys, values, out_weight):
        block = queries.shape[0]
        per_span = SPAN // block
        rank = lax.axis_index("seq").astype(jnp.int32).reshape(1)
        place = lax.axis_index("kv").astype(jnp.int32).reshape(1)
        kinds = min(3, max(2, seq // per_span))
        tables = rope_tables(block)
        by_head = jnp.transpose(queries, (1, 0, 2))
        pieces = {0: prepare(rank, keys[:, 0, :], values[:, 0, :], tables)}

        def fetch(offset, *others):
            if offset not in pieces:
                low = offset % per_span
                step = (low & -low) if low else offset & -offset
                if offset > per_span and low == 3:
                    step = 3
                source = fetch(offset - step)
                pieces[offset] = swap(after(source, *others) if others else source, "seq", seq, step)
            return pieces[offset]

        for offset in [step for step in (4, 8, 16, 32) if step < seq] + [2, 1]:
            fetch(offset)
        rot, *state, mine = begin(
            kinds, rank, place, by_head, tables, out_weight, pieces[0]
        )
        twin_weight = swap(out_weight, "kv", kv, 1)
        for offset in [3, 7, 6, 5] + list(range(seq)):
            fetch(offset, state[0])
        calls = [[1, 2, 3, 4]]
        while calls[-1][-1] < seq - 1:
            at = calls[-1][-1] + 1
            calls.append(list(range(at, min(at + per_span, seq))))
        for at, offsets in enumerate(calls[:-1]):
            stage = (place, twin_weight) if at == 0 else ()
            state = attend(
                rank, offsets, rot, [pieces[o] for o in offsets], state, False, 0, block, stage
            )
            if stage:
                *state, theirs = state
        parts = []
        offsets = calls[-1]
        rows = block // ROW_CHUNKS
        for chunk in range(ROW_CHUNKS):
            own = attend(
                rank, offsets, rot, [pieces[o] for o in offsets], state, True, chunk * rows, rows
            )
            twin = swap(own, "kv", kv, 1)
            away = project(1, own, twin, mine, theirs, jnp.bfloat16)
            landed = swap(away, "kv", kv, 2)
            home = project(0, own, twin, mine, theirs, jnp.float32)
            parts.append((home, landed))
        return close(parts)

    return shards


def solution(mesh):
    return jax.shard_map(
        make_shards(mesh.shape["seq"], mesh.shape["kv"]),
        mesh=mesh,
        in_specs=(P("seq", "kv", None), P("seq", "kv", None), P("seq", "kv", None), P("kv", None)),
        out_specs=P("seq", "kv"),
        check_vma=False,
    )
```

```python
import functools
import math

import jax
import jax.numpy as jnp
import numpy as np
from jax import lax
from jax.experimental import pallas as pl
from jax.experimental.pallas import tpu as pltpu
from jax.sharding import PartitionSpec as P

HEAD = 128
GROUP = 7
SPAN = 1024
LOCAL = 32
THETA = 10000000.0
NEG = -1e30
SCALE = math.log2(math.e) / math.sqrt(HEAD)
ROW_CHUNKS = (128, 128)
FIRST = [4, 1, 2, 3]
CALLS = [[1, 2], [3, 4], [7], [5, 6]]
LATER = [7, 6, 5]
EARLY = 0
STAGE = 1
VMEM = pltpu.MemorySpace.VMEM
HBM = pltpu.MemorySpace.HBM
LIMIT = 24 * 2**20
LIGHT = pl.CostEstimate(flops=1, bytes_accessed=1, transcendentals=0)


def rope_tables(block):
    inverse = np.exp(np.arange(HEAD // 2, dtype=np.float64) * (-2.0 * math.log(THETA) / HEAD))
    inner = np.arange(SPAN)
    first = np.minimum(np.arange(block) + SPAN, SPAN + LOCAL)
    far = np.full((block,), SPAN + LOCAL)
    angles = np.concatenate([inner, first, far])[:, None] * inverse
    cosine, sine = np.cos(angles), np.sin(angles)
    return (
        jnp.asarray(np.concatenate([cosine, cosine], 1), jnp.float32),
        jnp.asarray(np.concatenate([-sine, sine], 1), jnp.float32),
    )


def rotated(x, cosine, sine):
    x = x.astype(jnp.float32)
    return x * cosine + pltpu.roll(x, HEAD // 2, 1) * sine


def in_hbm(x):
    return pltpu.with_memory_space_constraint(x, HBM)


def prepare_kernel(rank_ref, key_hbm, value_hbm, cos_hbm, sin_hbm, out_ref, key_ref, cos_ref, sin_ref, sems):
    block = key_ref.shape[0]
    rows = pl.ds(pl.multiple_of(rank_ref[0] % (SPAN // block) * block, block), block)
    copies = [
        pltpu.make_async_copy(key_hbm, key_ref, sems.at[0]),
        pltpu.make_async_copy(cos_hbm.at[rows], cos_ref, sems.at[1]),
        pltpu.make_async_copy(sin_hbm.at[rows], sin_ref, sems.at[2]),
        pltpu.make_async_copy(value_hbm, out_ref.at[pl.ds(block, block)], sems.at[3]),
    ]
    for copy in copies:
        copy.start()
    for copy in copies:
        copy.wait()
    out_ref[:block] = rotated(key_ref[...], cos_ref[...], sin_ref[...]).astype(jnp.bfloat16)


def prepare(rank, keys, values, tables):
    block = keys.shape[0]
    return pl.pallas_call(
        prepare_kernel,
        in_specs=[pl.BlockSpec(memory_space=pltpu.SMEM)] + [pl.BlockSpec(memory_space=HBM)] * 4,
        out_specs=pl.BlockSpec(memory_space=VMEM),
        out_shape=jax.ShapeDtypeStruct((2 * block, HEAD), jnp.bfloat16),
        scratch_shapes=[
            pltpu.VMEM((block, HEAD), jnp.bfloat16),
            pltpu.VMEM((block, HEAD), jnp.float32),
            pltpu.VMEM((block, HEAD), jnp.float32),
            pltpu.SemaphoreType.DMA((4,)),
        ],
        compiler_params=pltpu.CompilerParams(vmem_limit_bytes=LIMIT),
        name="rotate_keys",
    )(rank, *[in_hbm(x) for x in (keys, values, *tables)])


def scores_of(query, pieces):
    block = pieces[0].shape[0] // 2
    return [
        lax.dot_general(
            q, piece[:block], (((1,), (1,)), ((), ())), preferred_element_type=jnp.float32
        )
        for q, piece in zip(query, pieces)
    ]


def absorb(scores, lifts, pieces, old):
    block = pieces[0].shape[0] // 2
    lanes = [slice(at, at + HEAD) for at in range(0, block, HEAD)]
    peak = None
    for score, lift in zip(scores, lifts):
        high = functools.reduce(jnp.maximum, [score[:, lane] for lane in lanes])
        if lift is not None:
            high = high - lift
        peak = high if peak is None else jnp.maximum(peak, high)
    top = jnp.max(peak, axis=1, keepdims=True)
    if old is None:
        top = jnp.broadcast_to(top, peak.shape)
        acc, total = None, None
    else:
        top = jnp.maximum(top, old[0])
        factor = jnp.exp2(old[0] - top)
        acc, total = factor * old[1], factor * old[2]
    ones = jnp.ones((block, HEAD), jnp.bfloat16)
    for score, lift, piece in zip(scores, lifts, pieces):
        base = top if lift is None else top + lift
        weight = jnp.exp2(score - jnp.concatenate([base] * len(lanes), 1)).astype(jnp.bfloat16)
        both = jnp.dot(
            weight, jnp.concatenate([piece[block:], ones], 1), preferred_element_type=jnp.float32
        )
        acc = both[:, :HEAD] if acc is None else acc + both[:, :HEAD]
        total = both[:, HEAD:] if total is None else total + both[:, HEAD:]
    return top, acc, total


def column_copies(place, weight_hbm, into, sems):
    columns = into[0].shape[1]
    copies = []
    for flip, ref in enumerate(into):
        at = pl.ds(pl.multiple_of((place ^ (2 * flip)) * columns, columns), columns)
        copies.append(pltpu.make_async_copy(weight_hbm.at[:, at], ref, sems.at[flip]))
    return copies


def begin_kernel(
    kinds, rank_ref, place_ref, query_hbm, cos_hbm, sin_hbm, weight_hbm, piece_ref,
    rot_ref, top_ref, acc_ref, total_ref, *refs,
):
    *mine, query_ref, cos_ref, sin_ref, sems, weight_sems = refs
    heads, block, _ = query_ref.shape
    per_span = SPAN // block
    rank, place = rank_ref[0], place_ref[0]
    inner = rank % per_span
    places = [inner, jnp.where(inner == 0, per_span, per_span + 1), per_span + 1][:kinds]
    copies = [pltpu.make_async_copy(query_hbm, query_ref, sems.at[0])]
    for kind, at in enumerate(places):
        rows = pl.ds(pl.multiple_of(at * block, block), block)
        copies.append(pltpu.make_async_copy(cos_hbm.at[rows], cos_ref.at[kind], sems.at[1 + 2 * kind]))
        copies.append(pltpu.make_async_copy(sin_hbm.at[rows], sin_ref.at[kind], sems.at[2 + 2 * kind]))
    for copy in copies:
        copy.start()
    loads = column_copies(place, weight_hbm, mine, weight_sems)
    for copy in loads:
        copy.start()
    for copy in copies:
        copy.wait()
    causal = lax.broadcasted_iota(jnp.int32, (block, block), 1) <= lax.broadcasted_iota(
        jnp.int32, (block, block), 0
    )
    for head in range(heads):
        for kind in range(kinds):
            rot_ref[kind, head] = (
                rotated(query_ref[head], cos_ref[kind], sin_ref[kind]) * SCALE
            ).astype(jnp.bfloat16)
    later = scores_of([rot_ref[0, 0]], [piece_ref])
    for head in range(heads):
        now = later
        if head + 1 < heads:
            later = scores_of([rot_ref[0, head + 1]], [piece_ref])
        now = [jnp.where(causal, now[0], NEG)]
        top_ref[head], acc_ref[head], total_ref[head] = absorb(now, [None], [piece_ref], None)
    for copy in loads:
        copy.wait()


def begin(kinds, rank, place, queries, tables, out_weight, piece):
    heads, block, _ = queries.shape
    depth = out_weight.shape[0]
    smem, hbm, vmem = (pl.BlockSpec(memory_space=space) for space in (pltpu.SMEM, HBM, VMEM))
    parts = 2
    return pl.pallas_call(
        functools.partial(begin_kernel, kinds),
        in_specs=[smem, smem, hbm, hbm, hbm, hbm, vmem],
        out_specs=[vmem] * (4 + parts),
        out_shape=[
            jax.ShapeDtypeStruct((kinds, heads, block, HEAD), jnp.bfloat16),
            *[jax.ShapeDtypeStruct((heads, block, HEAD), jnp.float32)] * 3,
            *[jax.ShapeDtypeStruct((depth, depth), jnp.bfloat16)] * parts,
        ],
        scratch_shapes=[
            pltpu.VMEM((heads, block, HEAD), jnp.bfloat16),
            pltpu.VMEM((kinds, block, HEAD), jnp.float32),
            pltpu.VMEM((kinds, block, HEAD), jnp.float32),
            pltpu.SemaphoreType.DMA((1 + 2 * kinds,)),
            pltpu.SemaphoreType.DMA((parts,)),
        ],
        cost_estimate=LIGHT,
        compiler_params=pltpu.CompilerParams(vmem_limit_bytes=LIMIT),
        name="attend_0",
    )(rank, place, *[in_hbm(x) for x in (queries, *tables, out_weight)], piece)


def attend_kernel(offsets, kinds, last, start, rows, stages, rank_ref, rot_ref, *refs):
    pieces, refs = refs[: len(offsets)], refs[len(offsets) :]
    old, refs = refs[:3], refs[3:]
    loads = []
    if stages:
        place_ref, weight_hbm, *refs, away_ref, sems = refs
        loads = column_copies(place_ref[0] ^ 2, weight_hbm, [away_ref], sems)
    for copy in loads:
        copy.start()
    block = pieces[0].shape[0] // 2
    per_span = SPAN // block
    rank = rank_ref[0]
    lifts = [jnp.where((rank ^ offset) <= rank, 0.0, -NEG).astype(jnp.float32) for offset in offsets]
    picked = []
    for offset in offsets:
        kind = min(offset // per_span, 1)
        if kind and kinds > 2:
            back = rank // per_span - (rank ^ offset) // per_span
            kind = jnp.clip(back, 1, kinds - 1)
        picked.append(kind)
    here = slice(start, start + rows)
    def scores_at(head):
        return scores_of([rot_ref[kind, head, here] for kind in picked], pieces)

    later = scores_at(0)
    for head in range(GROUP):
        now = later
        if head + 1 < GROUP:
            later = scores_at(head + 1)
        top, acc, total = absorb(now, lifts, pieces, [ref[head, here] for ref in old])
        if last:
            (out_ref,) = refs
            out_ref[:, head * HEAD : (head + 1) * HEAD] = (acc / total).astype(jnp.bfloat16)
        else:
            refs[0][head], refs[1][head], refs[2][head] = top, acc, total
    for copy in loads:
        copy.wait()


def attend(rank, offsets, rot, pieces, state, last, start, rows, stage=()):
    block = pieces[0].shape[0] // 2
    smem, vmem = (pl.BlockSpec(memory_space=space) for space in (pltpu.SMEM, VMEM))
    if last:
        out_specs = vmem
        out_shape = jax.ShapeDtypeStruct((rows, GROUP * HEAD), jnp.bfloat16)
    else:
        out_specs = [vmem] * 3
        out_shape = [jax.ShapeDtypeStruct((GROUP, rows, HEAD), jnp.float32)] * 3
    args, in_specs, scratch = [], [], []
    if stage:
        place, weight = stage
        depth = weight.shape[0]
        args = [place, in_hbm(weight)]
        in_specs = [smem, pl.BlockSpec(memory_space=HBM)]
        out_specs = [*out_specs, vmem]
        out_shape = [*out_shape, jax.ShapeDtypeStruct((depth, depth), jnp.bfloat16)]
        scratch = [pltpu.SemaphoreType.DMA((1,))]
    return pl.pallas_call(
        functools.partial(
            attend_kernel, tuple(offsets), rot.shape[0], last, start, rows, bool(stage)
        ),
        in_specs=[smem] + [vmem] * (4 + len(pieces)) + in_specs,
        scratch_shapes=scratch,
        out_specs=out_specs,
        out_shape=out_shape,
        cost_estimate=LIGHT,
        compiler_params=pltpu.CompilerParams(vmem_limit_bytes=LIMIT),
        name="attend_" + "_".join(map(str, offsets)),
    )(rank, rot, *pieces, *state, *args)


def project_kernel(own_ref, twin_ref, own_weight, twin_weight, out_ref):
    out_ref[...] = (
        jnp.dot(own_ref[...], own_weight[...], preferred_element_type=jnp.float32)
        + jnp.dot(twin_ref[...], twin_weight[...], preferred_element_type=jnp.float32)
    ).astype(out_ref.dtype)


def project(own, twin, own_weight, twin_weight, dtype, name):
    vmem = pl.BlockSpec(memory_space=VMEM)
    return pl.pallas_call(
        project_kernel,
        in_specs=[vmem] * 4,
        out_specs=vmem,
        out_shape=jax.ShapeDtypeStruct((own.shape[0], own_weight.shape[1]), dtype),
        cost_estimate=LIGHT,
        compiler_params=pltpu.CompilerParams(vmem_limit_bytes=LIMIT),
        name=name,
    )(own, twin, own_weight, twin_weight)


def home_kernel(count, place_ref, twin_hbm, own_weight, *refs):
    own_refs, twin_refs, refs = refs[:count], refs[count : 2 * count], refs[2 * count :]
    out_ref, twin_weight, sems = refs
    (load,) = column_copies(place_ref[0], twin_hbm, [twin_weight], sems)
    load.start()
    start = 0
    for own in own_refs:
        rows = pl.ds(start, own.shape[0])
        out_ref[rows] = jnp.dot(own[...], own_weight[...], preferred_element_type=jnp.float32)
        start += own.shape[0]
    load.wait()
    start = 0
    for twin in twin_refs:
        rows = pl.ds(start, twin.shape[0])
        out_ref[rows] += jnp.dot(twin[...], twin_weight[...], preferred_element_type=jnp.float32)
        start += twin.shape[0]


def project_home(place, own, twin, own_weight, twin_weight):
    smem, hbm, vmem = (pl.BlockSpec(memory_space=space) for space in (pltpu.SMEM, HBM, VMEM))
    rows = sum(x.shape[0] for x in own)
    return pl.pallas_call(
        functools.partial(home_kernel, len(own)),
        in_specs=[smem, hbm] + [vmem] * (2 * len(own) + 1),
        out_specs=vmem,
        out_shape=jax.ShapeDtypeStruct((rows, own_weight.shape[1]), jnp.float32),
        scratch_shapes=[
            pltpu.VMEM(own_weight.shape, jnp.bfloat16),
            pltpu.SemaphoreType.DMA((1,)),
        ],
        cost_estimate=LIGHT,
        compiler_params=pltpu.CompilerParams(vmem_limit_bytes=LIMIT),
        name="home",
    )(place, in_hbm(twin_weight), own_weight, *own, *twin)


def close_kernel(home_ref, *refs):
    *landed_refs, out_hbm, sum_ref, sems = refs
    copies, start = [], 0
    for at, landed in enumerate(landed_refs):
        rows = pl.ds(start, landed.shape[0])
        sum_ref[rows] = (home_ref[rows] + landed[...].astype(jnp.float32)).astype(sum_ref.dtype)
        copies.append(pltpu.make_async_copy(sum_ref.at[rows], out_hbm.at[rows], sems.at[at]))
        copies[-1].start()
        start += landed.shape[0]
    for copy in copies:
        copy.wait()


def close(home, landed):
    vmem, hbm = (pl.BlockSpec(memory_space=space) for space in (VMEM, HBM))
    return pl.pallas_call(
        close_kernel,
        in_specs=[vmem] * (1 + len(landed)),
        out_specs=hbm,
        out_shape=jax.ShapeDtypeStruct(home.shape, jnp.bfloat16),
        scratch_shapes=[
            pltpu.VMEM(home.shape, jnp.bfloat16),
            pltpu.SemaphoreType.DMA((len(landed),)),
        ],
        cost_estimate=LIGHT,
        compiler_params=pltpu.CompilerParams(vmem_limit_bytes=LIMIT),
        name="close",
    )(home, *landed)


def swap(x, axis, size, bits):
    return lax.ppermute(x, axis, [(i, i ^ bits) for i in range(size)])


def after(x, *others):
    return lax.optimization_barrier((x, *others))[0]


def make_shards(seq, kv):
    def shards(queries, keys, values, out_weight):
        block = queries.shape[0]
        per_span = SPAN // block
        rank = lax.axis_index("seq").astype(jnp.int32).reshape(1)
        place = lax.axis_index("kv").astype(jnp.int32).reshape(1)
        kinds = min(3, max(2, seq // per_span))
        tables = rope_tables(block)
        by_head = jnp.transpose(queries, (1, 0, 2))
        pieces = {0: prepare(rank, keys[:, 0, :], values[:, 0, :], tables)}

        def send(offset, step, *others):
            pieces[offset] = swap(after(pieces[offset ^ step], *others), "seq", seq, step)

        twin_weight = swap(out_weight, "kv", kv, 1)
        for offset in FIRST:
            send(offset, offset)
        rot, *state = begin(
            kinds, rank, place, by_head, tables, out_weight, pieces[0]
        )
        state, mine = state[:3], state[3:]
        for offset in range(2 * per_span, seq, per_span):
            send(offset, offset & -offset)
            for low in range(1, per_span):
                send(offset + low, low)
        calls = CALLS + [list(range(at, at + per_span)) for at in range(2 * per_span, seq, per_span)]

        def blocks(offsets, state, *how):
            return attend(rank, offsets, rot, [pieces[o] for o in offsets], state, *how)

        for at, offsets in enumerate(calls[:-1]):
            if at == EARLY:
                for offset in LATER:
                    send(offset, offset % per_span, state[0])
            state = blocks(offsets, state, False, 0, block, (place, twin_weight) if at == STAGE else ())
            if at == STAGE:
                state, theirs = state[:3], state[3]
        own, twin, start = [], [], 0
        for rows in ROW_CHUNKS:
            own.append(blocks(calls[-1], state, True, start, rows))
            twin.append(swap(own[-1], "kv", kv, 1))
            start += rows
        landed = []
        for rows in zip(own, twin):
            away = project(
                *rows, mine[1], theirs, jnp.bfloat16, "away"
            )
            landed.append(swap(away, "kv", kv, 2))
        home = project_home(place, own, twin, mine[0], twin_weight)
        return close(home, landed)

    return shards


def solution(mesh):
    return jax.shard_map(
        make_shards(mesh.shape["seq"], mesh.shape["kv"]),
        mesh=mesh,
        in_specs=(P("seq", "kv", None), P("seq", "kv", None), P("seq", "kv", None), P("kv", None)),
        out_specs=P("seq", "kv"),
        check_vma=False,
    )
```

```python
import functools
import math

import jax
import jax.numpy as jnp
import numpy as np
from jax import lax
from jax.experimental import pallas as pl
from jax.experimental.pallas import tpu as pltpu
from jax.sharding import PartitionSpec as P

HEAD = 128
GROUP = 7
SPAN = 1024
LOCAL = 32
THETA = 10000000.0
NEG = -1e30
SCALE = math.log2(math.e) / math.sqrt(HEAD)
ROW_CHUNKS = (128, 128)
TURN = 4
FIRST = [4, 1, 2, 3]
CALLS = [[0, 1], [2, 3], [4, 7], [5, 6]]
LATER = [7, 6, 5]
STAGES = [[0], [1]]
VMEM = pltpu.MemorySpace.VMEM
HBM = pltpu.MemorySpace.HBM
LIMIT = 24 * 2**20
LIGHT = pl.CostEstimate(flops=1, bytes_accessed=1, transcendentals=0)


def rope_tables(block):
    inverse = np.exp(np.arange(HEAD // 2, dtype=np.float64) * (-2.0 * math.log(THETA) / HEAD))
    inner = np.arange(SPAN)
    first = np.minimum(np.arange(block) + SPAN, SPAN + LOCAL)
    far = np.full((block,), SPAN + LOCAL)
    angles = np.concatenate([inner, first, far])[:, None] * inverse
    cosine, sine = np.cos(angles), np.sin(angles)
    return (
        jnp.asarray(np.concatenate([cosine, cosine], 1), jnp.float32),
        jnp.asarray(np.concatenate([-sine, sine], 1), jnp.float32),
    )


def rotated(x, cosine, sine):
    x = x.astype(jnp.float32)
    return x * cosine + pltpu.roll(x, HEAD // 2, 1) * sine


def in_hbm(x):
    return pltpu.with_memory_space_constraint(x, HBM)


def prepare_kernel(rank_ref, key_hbm, value_hbm, cos_hbm, sin_hbm, out_ref, key_ref, cos_ref, sin_ref, sems):
    block = key_ref.shape[0]
    rows = pl.ds(pl.multiple_of(rank_ref[0] % (SPAN // block) * block, block), block)
    copies = [
        pltpu.make_async_copy(key_hbm, key_ref, sems.at[0]),
        pltpu.make_async_copy(cos_hbm.at[rows], cos_ref, sems.at[1]),
        pltpu.make_async_copy(sin_hbm.at[rows], sin_ref, sems.at[2]),
        pltpu.make_async_copy(value_hbm, out_ref.at[pl.ds(block, block)], sems.at[3]),
    ]
    for copy in copies:
        copy.start()
    for copy in copies:
        copy.wait()
    out_ref[:block] = rotated(key_ref[...], cos_ref[...], sin_ref[...]).astype(jnp.bfloat16)


def prepare(rank, keys, values, tables):
    block = keys.shape[0]
    return pl.pallas_call(
        prepare_kernel,
        in_specs=[pl.BlockSpec(memory_space=pltpu.SMEM)] + [pl.BlockSpec(memory_space=HBM)] * 4,
        out_specs=pl.BlockSpec(memory_space=VMEM),
        out_shape=jax.ShapeDtypeStruct((2 * block, HEAD), jnp.bfloat16),
        scratch_shapes=[
            pltpu.VMEM((block, HEAD), jnp.bfloat16),
            pltpu.VMEM((block, HEAD), jnp.float32),
            pltpu.VMEM((block, HEAD), jnp.float32),
            pltpu.SemaphoreType.DMA((4,)),
        ],
        compiler_params=pltpu.CompilerParams(vmem_limit_bytes=LIMIT),
        name="rotate_keys",
    )(rank, *[in_hbm(x) for x in (keys, values, *tables)])


def scores_of(query, pieces):
    block = pieces[0].shape[0] // 2
    return [
        lax.dot_general(
            q, piece[:block], (((1,), (1,)), ((), ())), preferred_element_type=jnp.float32
        )
        for q, piece in zip(query, pieces)
    ]


def absorb(scores, lifts, pieces, old):
    block = pieces[0].shape[0] // 2
    lanes = [slice(at, at + HEAD) for at in range(0, block, HEAD)]
    peak = None
    for score, lift in zip(scores, lifts):
        high = functools.reduce(jnp.maximum, [score[:, lane] for lane in lanes])
        if lift is not None:
            high = high - lift
        peak = high if peak is None else jnp.maximum(peak, high)
    top = jnp.max(peak, axis=1, keepdims=True)
    if old is None:
        top = jnp.broadcast_to(top, peak.shape)
        acc, total = None, None
    else:
        top = jnp.maximum(top, old[0])
        factor = jnp.exp2(old[0] - top)
        acc, total = factor * old[1], factor * old[2]
    ones = jnp.ones((block, HEAD), jnp.bfloat16)
    for score, lift, piece in zip(scores, lifts, pieces):
        base = top if lift is None else top + lift
        weight = jnp.exp2(score - jnp.concatenate([base] * len(lanes), 1)).astype(jnp.bfloat16)
        both = jnp.dot(
            weight, jnp.concatenate([piece[block:], ones], 1), preferred_element_type=jnp.float32
        )
        acc = both[:, :HEAD] if acc is None else acc + both[:, :HEAD]
        total = both[:, HEAD:] if total is None else total + both[:, HEAD:]
    return top, acc, total


def column_copies(place, weight_hbm, into, sems):
    columns = into[0].shape[1]
    copies = []
    for flip, ref in enumerate(into):
        at = pl.ds(pl.multiple_of((place ^ (2 * flip)) * columns, columns), columns)
        copies.append(pltpu.make_async_copy(weight_hbm.at[:, at], ref, sems.at[flip]))
    return copies


def turn_kernel(kinds, rank_ref, query_hbm, cos_hbm, sin_hbm, rot_ref, query_ref, cos_ref, sin_ref, sems):
    heads, block, _ = query_ref.shape
    per_span = SPAN // block
    inner = rank_ref[0] % per_span
    places = [inner, jnp.where(inner == 0, per_span, per_span + 1), per_span + 1][:kinds]
    copies = [pltpu.make_async_copy(query_hbm, query_ref, sems.at[0])]
    for kind, at in enumerate(places):
        rows = pl.ds(pl.multiple_of(at * block, block), block)
        copies.append(pltpu.make_async_copy(cos_hbm.at[rows], cos_ref.at[kind], sems.at[1 + 2 * kind]))
        copies.append(pltpu.make_async_copy(sin_hbm.at[rows], sin_ref.at[kind], sems.at[2 + 2 * kind]))
    for copy in copies:
        copy.start()
    for copy in copies:
        copy.wait()

    def turned(kind):
        for head in range(heads):
            rot_ref[kind, head] = (
                rotated(query_ref[head], cos_ref[kind], sin_ref[kind]) * SCALE
            ).astype(jnp.bfloat16)

    turned(0)
    for kind in range(1, kinds):
        pl.when(rank_ref[0] >= kind * per_span)(functools.partial(turned, kind))


def turn(kinds, rank, queries, tables):
    heads, block, _ = queries.shape
    smem, hbm, vmem = (pl.BlockSpec(memory_space=space) for space in (pltpu.SMEM, HBM, VMEM))
    return pl.pallas_call(
        functools.partial(turn_kernel, kinds),
        in_specs=[smem, hbm, hbm, hbm],
        out_specs=vmem,
        out_shape=jax.ShapeDtypeStruct((kinds, heads, block, HEAD), jnp.bfloat16),
        scratch_shapes=[
            pltpu.VMEM((heads, block, HEAD), jnp.bfloat16),
            pltpu.VMEM((kinds, block, HEAD), jnp.float32),
            pltpu.VMEM((kinds, block, HEAD), jnp.float32),
            pltpu.SemaphoreType.DMA((1 + 2 * kinds,)),
        ],
        cost_estimate=LIGHT,
        compiler_params=pltpu.CompilerParams(vmem_limit_bytes=LIMIT),
        name="rotate_queries",
    )(rank, *[in_hbm(x) for x in (queries, *tables)])


def attend_kernel(offsets, kinds, first, last, start, rows, stages, rank_ref, rot_ref, *refs):
    pieces, refs = refs[: len(offsets)], refs[len(offsets) :]
    old, refs = ([], refs) if first else (refs[:3], refs[3:])
    loads = []
    if stages:
        place_ref, *refs, sems = refs
        weights, refs, staged = refs[:stages], refs[stages:-stages], refs[-stages:]
        for at, (weight_hbm, ref) in enumerate(zip(weights, staged)):
            loads += column_copies(place_ref[0] ^ 2, weight_hbm, [ref], sems.at[pl.ds(at, 1)])
    for copy in loads:
        copy.start()
    block = pieces[0].shape[0] // 2
    per_span = SPAN // block
    rank = rank_ref[0]
    lifts = [
        jnp.where((rank ^ offset) <= rank, 0.0, -NEG).astype(jnp.float32) if offset else None
        for offset in offsets
    ]
    picked = []
    for offset in offsets:
        kind = min(offset // per_span, 1)
        if kind and kinds > 2:
            back = rank // per_span - (rank ^ offset) // per_span
            kind = jnp.clip(back, 1, kinds - 1)
        picked.append(kind)
    here = slice(start, start + rows)
    if 0 in offsets:
        causal = lax.broadcasted_iota(jnp.int32, (rows, block), 1) <= start + lax.broadcasted_iota(
            jnp.int32, (rows, block), 0
        )

    def scores_at(head):
        scores = scores_of([rot_ref[kind, head, here] for kind in picked], pieces)
        return [
            score if offset else jnp.where(causal, score, NEG)
            for offset, score in zip(offsets, scores)
        ]

    def put(head, top, acc, total):
        if last:
            refs[0][:, head * HEAD : (head + 1) * HEAD] = (acc / total).astype(jnp.bfloat16)
        else:
            refs[0][head], refs[1][head], refs[2][head] = top, acc, total

    def meet():
        later = scores_at(0)
        for head in range(GROUP):
            now = later
            if head + 1 < GROUP:
                later = scores_at(head + 1)
            put(
                head,
                *absorb(now, lifts, pieces, [ref[head, here] for ref in old] or None),
            )

    def keep():
        for head in range(GROUP):
            put(head, *[ref[head, here] for ref in old])

    if first:
        meet()
    else:
        seen = functools.reduce(jnp.logical_or, [(rank ^ offset) <= rank for offset in offsets])
        pl.when(seen)(meet)
        pl.when(jnp.logical_not(seen))(keep)
    for copy in loads:
        copy.wait()


def attend(rank, offsets, rot, pieces, state, last, start, rows, stage=()):
    block = pieces[0].shape[0] // 2
    smem, vmem = (pl.BlockSpec(memory_space=space) for space in (pltpu.SMEM, VMEM))
    if last:
        out_specs = vmem
        out_shape = jax.ShapeDtypeStruct((rows, GROUP * HEAD), jnp.bfloat16)
    else:
        out_specs = [vmem] * 3
        out_shape = [jax.ShapeDtypeStruct((GROUP, rows, HEAD), jnp.float32)] * 3
    args, in_specs, scratch = [], [], []
    if stage:
        place, *weights = stage
        depth = weights[0].shape[0]
        args = [place, *[in_hbm(weight) for weight in weights]]
        in_specs = [smem] + [pl.BlockSpec(memory_space=HBM)] * len(weights)
        out_specs = [*out_specs, *[vmem] * len(weights)]
        out_shape = [
            *out_shape,
            *[jax.ShapeDtypeStruct((depth, depth), jnp.bfloat16)] * len(weights),
        ]
        scratch = [pltpu.SemaphoreType.DMA((len(weights),))]
    return pl.pallas_call(
        functools.partial(
            attend_kernel,
            tuple(offsets),
            rot.shape[0],
            not state,
            last,
            start,
            rows,
            len(stage[1:]),
        ),
        in_specs=[smem] + [vmem] * (1 + len(pieces) + len(state)) + in_specs,
        scratch_shapes=scratch,
        out_specs=out_specs,
        out_shape=out_shape,
        cost_estimate=LIGHT,
        compiler_params=pltpu.CompilerParams(vmem_limit_bytes=LIMIT),
        name="attend_" + "_".join(map(str, offsets)),
    )(rank, rot, *pieces, *state, *args)


def project_kernel(own_ref, twin_ref, own_weight, twin_weight, out_ref):
    out_ref[...] = (
        jnp.dot(own_ref[...], own_weight[...], preferred_element_type=jnp.float32)
        + jnp.dot(twin_ref[...], twin_weight[...], preferred_element_type=jnp.float32)
    ).astype(out_ref.dtype)


def project(own, twin, own_weight, twin_weight, dtype, name):
    vmem = pl.BlockSpec(memory_space=VMEM)
    return pl.pallas_call(
        project_kernel,
        in_specs=[vmem] * 4,
        out_specs=vmem,
        out_shape=jax.ShapeDtypeStruct((own.shape[0], own_weight.shape[1]), dtype),
        cost_estimate=LIGHT,
        compiler_params=pltpu.CompilerParams(vmem_limit_bytes=LIMIT),
        name=name,
    )(own, twin, own_weight, twin_weight)


def home_kernel(count, place_ref, own_hbm, twin_hbm, *refs):
    own_refs, twin_refs, refs = refs[:count], refs[count : 2 * count], refs[2 * count :]
    out_ref, own_weight, twin_weight, sems = refs
    loads = []
    for at, (hbm, ref) in enumerate(((own_hbm, own_weight), (twin_hbm, twin_weight))):
        loads += column_copies(place_ref[0], hbm, [ref], sems.at[pl.ds(at, 1)])
    for load in loads:
        load.start()
    for load in loads:
        load.wait()
    start = 0
    for own, twin in zip(own_refs, twin_refs):
        rows = pl.ds(start, own.shape[0])
        out_ref[rows] = jnp.dot(
            own[...], own_weight[...], preferred_element_type=jnp.float32
        ) + jnp.dot(twin[...], twin_weight[...], preferred_element_type=jnp.float32)
        start += own.shape[0]


def project_home(place, own, twin, own_weight, twin_weight):
    smem, hbm, vmem = (pl.BlockSpec(memory_space=space) for space in (pltpu.SMEM, HBM, VMEM))
    rows = sum(x.shape[0] for x in own)
    depth = own_weight.shape[0]
    return pl.pallas_call(
        functools.partial(home_kernel, len(own)),
        in_specs=[smem, hbm, hbm] + [vmem] * (2 * len(own)),
        out_specs=vmem,
        out_shape=jax.ShapeDtypeStruct((rows, depth), jnp.float32),
        scratch_shapes=[
            pltpu.VMEM((depth, depth), jnp.bfloat16),
            pltpu.VMEM((depth, depth), jnp.bfloat16),
            pltpu.SemaphoreType.DMA((2,)),
        ],
        cost_estimate=LIGHT,
        compiler_params=pltpu.CompilerParams(vmem_limit_bytes=LIMIT),
        name="home",
    )(place, in_hbm(own_weight), in_hbm(twin_weight), *own, *twin)


def close_kernel(home_ref, *refs):
    *landed_refs, out_hbm, sum_ref, sems = refs
    copies, start = [], 0
    for at, landed in enumerate(landed_refs):
        rows = pl.ds(start, landed.shape[0])
        sum_ref[rows] = (home_ref[rows] + landed[...].astype(jnp.float32)).astype(sum_ref.dtype)
        copies.append(pltpu.make_async_copy(sum_ref.at[rows], out_hbm.at[rows], sems.at[at]))
        copies[-1].start()
        start += landed.shape[0]
    for copy in copies:
        copy.wait()


def close(home, landed):
    vmem, hbm = (pl.BlockSpec(memory_space=space) for space in (VMEM, HBM))
    return pl.pallas_call(
        close_kernel,
        in_specs=[vmem] * (1 + len(landed)),
        out_specs=hbm,
        out_shape=jax.ShapeDtypeStruct(home.shape, jnp.bfloat16),
        scratch_shapes=[
            pltpu.VMEM(home.shape, jnp.bfloat16),
            pltpu.SemaphoreType.DMA((len(landed),)),
        ],
        cost_estimate=LIGHT,
        compiler_params=pltpu.CompilerParams(vmem_limit_bytes=LIMIT),
        name="close",
    )(home, *landed)


def swap(x, axis, size, bits):
    return lax.ppermute(x, axis, [(i, i ^ bits) for i in range(size)])


def after(x, *others):
    return lax.optimization_barrier((x, *others))[0]


def make_shards(seq, kv):
    def shards(queries, keys, values, out_weight):
        block = queries.shape[0]
        per_span = SPAN // block
        rank = lax.axis_index("seq").astype(jnp.int32).reshape(1)
        place = lax.axis_index("kv").astype(jnp.int32).reshape(1)
        kinds = min(3, max(2, seq // per_span))
        tables = rope_tables(block)
        by_head = jnp.transpose(queries, (1, 0, 2))
        pieces = {0: prepare(rank, keys[:, 0, :], values[:, 0, :], tables)}

        def send(offset, step, *others):
            pieces[offset] = swap(after(pieces[offset ^ step], *others), "seq", seq, step)

        twin_weight = swap(out_weight, "kv", kv, 1)
        for offset in FIRST:
            send(offset, offset)
        rot = turn(kinds, rank, by_head, tables)
        for offset in range(2 * per_span, seq, per_span):
            send(offset, offset & -offset)
            for low in range(1, per_span):
                send(offset + low, low)
        calls = CALLS + [list(range(at, at + per_span)) for at in range(2 * per_span, seq, per_span)]

        def blocks(offsets, state, *how):
            return attend(rank, offsets, rot, [pieces[o] for o in offsets], state, *how)

        for offset in LATER:
            send(offset, offset ^ TURN, rot)
        state, staged = [], []
        for offsets, weights in zip(calls[:-1], STAGES + [[]] * len(calls)):
            stage = (place, *[(out_weight, twin_weight)[at] for at in weights]) if weights else ()
            state = blocks(offsets, state, False, 0, block, stage)
            state, staged = state[:3], staged + list(state[3:])
        own, twin, start = [], [], 0
        for rows in ROW_CHUNKS:
            own.append(blocks(calls[-1], state, True, start, rows))
            twin.append(swap(own[-1], "kv", kv, 1))
            start += rows
        landed = []
        for rows in zip(own, twin):
            away = project(
                *rows, *staged, jnp.bfloat16, "away"
            )
            landed.append(swap(away, "kv", kv, 2))
        home = project_home(place, own, twin, out_weight, twin_weight)
        return close(home, landed)

    return shards


def solution(mesh):
    return jax.shard_map(
        make_shards(mesh.shape["seq"], mesh.shape["kv"]),
        mesh=mesh,
        in_specs=(P("seq", "kv", None), P("seq", "kv", None), P("seq", "kv", None), P("kv", None)),
        out_specs=P("seq", "kv"),
        check_vma=False,
    )
```

```python
import functools
import math

import jax
import jax.numpy as jnp
import numpy as np
from jax import lax
from jax.experimental import pallas as pl
from jax.experimental.pallas import tpu as pltpu
from jax.sharding import PartitionSpec as P

HEAD = 128
GROUP = 7
SPAN = 1024
LOCAL = 32
THETA = 10000000.0
NEG = -1e30
SCALE = math.log2(math.e) / math.sqrt(HEAD)
ROW_CHUNKS = (128, 128)
TURN = 6
FIRST = [6, 1, 2, 3]
CALLS = [[1, 2], [3, 6], [5], [4, 7]]
LATER = [5, 4, 7]
STAGES = [[], [1]]
VMEM = pltpu.MemorySpace.VMEM
HBM = pltpu.MemorySpace.HBM
LIMIT = 24 * 2**20
LIGHT = pl.CostEstimate(flops=1, bytes_accessed=1, transcendentals=0)


def rope_tables(block):
    inverse = np.exp(np.arange(HEAD // 2, dtype=np.float64) * (-2.0 * math.log(THETA) / HEAD))
    inner = np.arange(SPAN)
    first = np.minimum(np.arange(block) + SPAN, SPAN + LOCAL)
    far = np.full((block,), SPAN + LOCAL)
    angles = np.concatenate([inner, first, far])[:, None] * inverse
    cosine, sine = np.cos(angles), np.sin(angles)
    return (
        jnp.asarray(np.concatenate([cosine, cosine], 1), jnp.float32),
        jnp.asarray(np.concatenate([-sine, sine], 1), jnp.float32),
    )


def rotated(x, cosine, sine):
    x = x.astype(jnp.float32)
    return x * cosine + pltpu.roll(x, HEAD // 2, 1) * sine


def in_hbm(x):
    return pltpu.with_memory_space_constraint(x, HBM)


def prepare_kernel(rank_ref, key_hbm, value_hbm, cos_hbm, sin_hbm, out_ref, key_ref, cos_ref, sin_ref, sems):
    block = key_ref.shape[0]
    rows = pl.ds(pl.multiple_of(rank_ref[0] % (SPAN // block) * block, block), block)
    copies = [
        pltpu.make_async_copy(key_hbm, key_ref, sems.at[0]),
        pltpu.make_async_copy(cos_hbm.at[rows], cos_ref, sems.at[1]),
        pltpu.make_async_copy(sin_hbm.at[rows], sin_ref, sems.at[2]),
        pltpu.make_async_copy(value_hbm, out_ref.at[pl.ds(block, block)], sems.at[3]),
    ]
    for copy in copies:
        copy.start()
    for copy in copies:
        copy.wait()
    out_ref[:block] = rotated(key_ref[...], cos_ref[...], sin_ref[...]).astype(jnp.bfloat16)


def prepare(rank, keys, values, tables):
    block = keys.shape[0]
    return pl.pallas_call(
        prepare_kernel,
        in_specs=[pl.BlockSpec(memory_space=pltpu.SMEM)] + [pl.BlockSpec(memory_space=HBM)] * 4,
        out_specs=pl.BlockSpec(memory_space=VMEM),
        out_shape=jax.ShapeDtypeStruct((2 * block, HEAD), jnp.bfloat16),
        scratch_shapes=[
            pltpu.VMEM((block, HEAD), jnp.bfloat16),
            pltpu.VMEM((block, HEAD), jnp.float32),
            pltpu.VMEM((block, HEAD), jnp.float32),
            pltpu.SemaphoreType.DMA((4,)),
        ],
        compiler_params=pltpu.CompilerParams(vmem_limit_bytes=LIMIT),
        name="rotate_keys",
    )(rank, *[in_hbm(x) for x in (keys, values, *tables)])


def scores_of(query, pieces):
    block = pieces[0].shape[0] // 2
    return [
        lax.dot_general(
            q, piece[:block], (((1,), (1,)), ((), ())), preferred_element_type=jnp.float32
        )
        for q, piece in zip(query, pieces)
    ]


def absorb(scores, lifts, pieces, old):
    block = pieces[0].shape[0] // 2
    lanes = [slice(at, at + HEAD) for at in range(0, block, HEAD)]
    peak = None
    for score, lift in zip(scores, lifts):
        high = functools.reduce(jnp.maximum, [score[:, lane] for lane in lanes])
        if lift is not None:
            high = high - lift
        peak = high if peak is None else jnp.maximum(peak, high)
    top = jnp.max(peak, axis=1, keepdims=True)
    if old is None:
        top = jnp.broadcast_to(top, peak.shape)
        acc, total = None, None
    else:
        top = jnp.maximum(top, old[0])
        factor = jnp.exp2(old[0] - top)
        acc, total = factor * old[1], factor * old[2]
    ones = jnp.ones((block, HEAD), jnp.bfloat16)
    for score, lift, piece in zip(scores, lifts, pieces):
        base = top if lift is None else top + lift
        weight = jnp.exp2(score - jnp.concatenate([base] * len(lanes), 1)).astype(jnp.bfloat16)
        both = jnp.dot(
            weight, jnp.concatenate([piece[block:], ones], 1), preferred_element_type=jnp.float32
        )
        acc = both[:, :HEAD] if acc is None else acc + both[:, :HEAD]
        total = both[:, HEAD:] if total is None else total + both[:, HEAD:]
    return top, acc, total


def column_copies(place, weight_hbm, into, sems):
    columns = into[0].shape[1]
    copies = []
    for flip, ref in enumerate(into):
        at = pl.ds(pl.multiple_of((place ^ (2 * flip)) * columns, columns), columns)
        copies.append(pltpu.make_async_copy(weight_hbm.at[:, at], ref, sems.at[flip]))
    return copies


def begin_kernel(
    kinds, rank_ref, place_ref, query_hbm, cos_hbm, sin_hbm, weight_hbm, piece_ref,
    rot_ref, top_ref, acc_ref, total_ref, *refs,
):
    away_ref, query_ref, cos_ref, sin_ref, sems, weight_sems = refs
    heads, block, _ = query_ref.shape
    per_span = SPAN // block
    rank, place = rank_ref[0], place_ref[0]
    inner = rank % per_span
    places = [inner, jnp.where(inner == 0, per_span, per_span + 1), per_span + 1][:kinds]
    copies = [pltpu.make_async_copy(query_hbm, query_ref, sems.at[0])]
    for kind, at in enumerate(places):
        rows = pl.ds(pl.multiple_of(at * block, block), block)
        copies.append(pltpu.make_async_copy(cos_hbm.at[rows], cos_ref.at[kind], sems.at[1 + 2 * kind]))
        copies.append(pltpu.make_async_copy(sin_hbm.at[rows], sin_ref.at[kind], sems.at[2 + 2 * kind]))
    for copy in copies:
        copy.start()
    loads = column_copies(place ^ 2, weight_hbm, [away_ref], weight_sems)
    for copy in loads:
        copy.start()
    for copy in copies:
        copy.wait()
    causal = lax.broadcasted_iota(jnp.int32, (block, block), 1) <= lax.broadcasted_iota(
        jnp.int32, (block, block), 0
    )
    def turn(kind):
        for head in range(heads):
            rot_ref[kind, head] = (
                rotated(query_ref[head], cos_ref[kind], sin_ref[kind]) * SCALE
            ).astype(jnp.bfloat16)

    turn(0)
    for kind in range(1, kinds):
        pl.when(rank >= kind * per_span)(functools.partial(turn, kind))
    later = scores_of([rot_ref[0, 0]], [piece_ref])
    for head in range(heads):
        now = later
        if head + 1 < heads:
            later = scores_of([rot_ref[0, head + 1]], [piece_ref])
        now = [jnp.where(causal, now[0], NEG)]
        top_ref[head], acc_ref[head], total_ref[head] = absorb(now, [None], [piece_ref], None)
    for copy in loads:
        copy.wait()


def begin(kinds, rank, place, queries, tables, out_weight, piece):
    heads, block, _ = queries.shape
    depth = out_weight.shape[0]
    smem, hbm, vmem = (pl.BlockSpec(memory_space=space) for space in (pltpu.SMEM, HBM, VMEM))
    return pl.pallas_call(
        functools.partial(begin_kernel, kinds),
        in_specs=[smem, smem, hbm, hbm, hbm, hbm, vmem],
        out_specs=[vmem] * 5,
        out_shape=[
            jax.ShapeDtypeStruct((kinds, heads, block, HEAD), jnp.bfloat16),
            *[jax.ShapeDtypeStruct((heads, block, HEAD), jnp.float32)] * 3,
            jax.ShapeDtypeStruct((depth, depth), jnp.bfloat16),
        ],
        scratch_shapes=[
            pltpu.VMEM((heads, block, HEAD), jnp.bfloat16),
            pltpu.VMEM((kinds, block, HEAD), jnp.float32),
            pltpu.VMEM((kinds, block, HEAD), jnp.float32),
            pltpu.SemaphoreType.DMA((1 + 2 * kinds,)),
            pltpu.SemaphoreType.DMA((1,)),
        ],
        cost_estimate=LIGHT,
        compiler_params=pltpu.CompilerParams(vmem_limit_bytes=LIMIT),
        name="attend_0",
    )(rank, place, *[in_hbm(x) for x in (queries, *tables, out_weight)], piece)


def attend_kernel(offsets, kinds, first, last, start, rows, stages, rank_ref, rot_ref, *refs):
    pieces, refs = refs[: len(offsets)], refs[len(offsets) :]
    old, refs = ([], refs) if first else (refs[:3], refs[3:])
    loads = []
    if stages:
        place_ref, *refs, sems = refs
        weights, refs, staged = refs[:stages], refs[stages:-stages], refs[-stages:]
        for at, (weight_hbm, ref) in enumerate(zip(weights, staged)):
            loads += column_copies(place_ref[0] ^ 2, weight_hbm, [ref], sems.at[pl.ds(at, 1)])
    for copy in loads:
        copy.start()
    block = pieces[0].shape[0] // 2
    per_span = SPAN // block
    rank = rank_ref[0]
    lifts = [
        jnp.where((rank ^ offset) <= rank, 0.0, -NEG).astype(jnp.float32) if offset else None
        for offset in offsets
    ]
    picked = []
    for offset in offsets:
        kind = min(offset // per_span, 1)
        if kind and kinds > 2:
            back = rank // per_span - (rank ^ offset) // per_span
            kind = jnp.clip(back, 1, kinds - 1)
        picked.append(kind)
    here = slice(start, start + rows)
    if 0 in offsets:
        causal = lax.broadcasted_iota(jnp.int32, (rows, block), 1) <= start + lax.broadcasted_iota(
            jnp.int32, (rows, block), 0
        )

    def scores_at(head):
        scores = scores_of([rot_ref[kind, head, here] for kind in picked], pieces)
        return [
            score if offset else jnp.where(causal, score, NEG)
            for offset, score in zip(offsets, scores)
        ]

    def put(head, top, acc, total):
        if last:
            refs[0][:, head * HEAD : (head + 1) * HEAD] = (acc / total).astype(jnp.bfloat16)
        else:
            refs[0][head], refs[1][head], refs[2][head] = top, acc, total

    def meet():
        later = scores_at(0)
        for head in range(GROUP):
            now = later
            if head + 1 < GROUP:
                later = scores_at(head + 1)
            put(
                head,
                *absorb(now, lifts, pieces, [ref[head, here] for ref in old] or None),
            )

    def keep():
        for head in range(GROUP):
            put(head, *[ref[head, here] for ref in old])

    if first:
        meet()
    else:
        seen = functools.reduce(jnp.logical_or, [(rank ^ offset) <= rank for offset in offsets])
        pl.when(seen)(meet)
        pl.when(jnp.logical_not(seen))(keep)
    for copy in loads:
        copy.wait()


def attend(rank, offsets, rot, pieces, state, last, start, rows, stage=()):
    block = pieces[0].shape[0] // 2
    smem, vmem = (pl.BlockSpec(memory_space=space) for space in (pltpu.SMEM, VMEM))
    if last:
        out_specs = vmem
        out_shape = jax.ShapeDtypeStruct((rows, GROUP * HEAD), jnp.bfloat16)
    else:
        out_specs = [vmem] * 3
        out_shape = [jax.ShapeDtypeStruct((GROUP, rows, HEAD), jnp.float32)] * 3
    args, in_specs, scratch = [], [], []
    if stage:
        place, *weights = stage
        depth = weights[0].shape[0]
        args = [place, *[in_hbm(weight) for weight in weights]]
        in_specs = [smem] + [pl.BlockSpec(memory_space=HBM)] * len(weights)
        out_specs = [*out_specs, *[vmem] * len(weights)]
        out_shape = [
            *out_shape,
            *[jax.ShapeDtypeStruct((depth, depth), jnp.bfloat16)] * len(weights),
        ]
        scratch = [pltpu.SemaphoreType.DMA((len(weights),))]
    return pl.pallas_call(
        functools.partial(
            attend_kernel,
            tuple(offsets),
            rot.shape[0],
            not state,
            last,
            start,
            rows,
            len(stage[1:]),
        ),
        in_specs=[smem] + [vmem] * (1 + len(pieces) + len(state)) + in_specs,
        scratch_shapes=scratch,
        out_specs=out_specs,
        out_shape=out_shape,
        cost_estimate=LIGHT,
        compiler_params=pltpu.CompilerParams(vmem_limit_bytes=LIMIT),
        name="attend_" + "_".join(map(str, offsets)),
    )(rank, rot, *pieces, *state, *args)


def project_kernel(own_ref, twin_ref, own_weight, twin_weight, out_ref):
    out_ref[...] = (
        jnp.dot(own_ref[...], own_weight[...], preferred_element_type=jnp.float32)
        + jnp.dot(twin_ref[...], twin_weight[...], preferred_element_type=jnp.float32)
    ).astype(out_ref.dtype)


def project(own, twin, own_weight, twin_weight, dtype, name):
    vmem = pl.BlockSpec(memory_space=VMEM)
    return pl.pallas_call(
        project_kernel,
        in_specs=[vmem] * 4,
        out_specs=vmem,
        out_shape=jax.ShapeDtypeStruct((own.shape[0], own_weight.shape[1]), dtype),
        cost_estimate=LIGHT,
        compiler_params=pltpu.CompilerParams(vmem_limit_bytes=LIMIT),
        name=name,
    )(own, twin, own_weight, twin_weight)


def home_kernel(count, place_ref, own_hbm, twin_hbm, *refs):
    own_refs, twin_refs, refs = refs[:count], refs[count : 2 * count], refs[2 * count :]
    out_ref, own_weight, twin_weight, sems = refs
    loads = []
    for at, (hbm, ref) in enumerate(((own_hbm, own_weight), (twin_hbm, twin_weight))):
        loads += column_copies(place_ref[0], hbm, [ref], sems.at[pl.ds(at, 1)])
    for load in loads:
        load.start()
    for load in loads:
        load.wait()
    start = 0
    for own, twin in zip(own_refs, twin_refs):
        rows = pl.ds(start, own.shape[0])
        out_ref[rows] = jnp.dot(
            own[...], own_weight[...], preferred_element_type=jnp.float32
        ) + jnp.dot(twin[...], twin_weight[...], preferred_element_type=jnp.float32)
        start += own.shape[0]


def project_home(place, own, twin, own_weight, twin_weight):
    smem, hbm, vmem = (pl.BlockSpec(memory_space=space) for space in (pltpu.SMEM, HBM, VMEM))
    rows = sum(x.shape[0] for x in own)
    depth = own_weight.shape[0]
    return pl.pallas_call(
        functools.partial(home_kernel, len(own)),
        in_specs=[smem, hbm, hbm] + [vmem] * (2 * len(own)),
        out_specs=vmem,
        out_shape=jax.ShapeDtypeStruct((rows, depth), jnp.float32),
        scratch_shapes=[
            pltpu.VMEM((depth, depth), jnp.bfloat16),
            pltpu.VMEM((depth, depth), jnp.bfloat16),
            pltpu.SemaphoreType.DMA((2,)),
        ],
        cost_estimate=LIGHT,
        compiler_params=pltpu.CompilerParams(vmem_limit_bytes=LIMIT),
        name="home",
    )(place, in_hbm(own_weight), in_hbm(twin_weight), *own, *twin)


def close_kernel(home_ref, *refs):
    *landed_refs, out_hbm, sum_ref, sems = refs
    copies, start = [], 0
    for at, landed in enumerate(landed_refs):
        rows = pl.ds(start, landed.shape[0])
        sum_ref[rows] = (home_ref[rows] + landed[...].astype(jnp.float32)).astype(sum_ref.dtype)
        copies.append(pltpu.make_async_copy(sum_ref.at[rows], out_hbm.at[rows], sems.at[at]))
        copies[-1].start()
        start += landed.shape[0]
    for copy in copies:
        copy.wait()


def close(home, landed):
    vmem, hbm = (pl.BlockSpec(memory_space=space) for space in (VMEM, HBM))
    return pl.pallas_call(
        close_kernel,
        in_specs=[vmem] * (1 + len(landed)),
        out_specs=hbm,
        out_shape=jax.ShapeDtypeStruct(home.shape, jnp.bfloat16),
        scratch_shapes=[
            pltpu.VMEM(home.shape, jnp.bfloat16),
            pltpu.SemaphoreType.DMA((len(landed),)),
        ],
        cost_estimate=LIGHT,
        compiler_params=pltpu.CompilerParams(vmem_limit_bytes=LIMIT),
        name="close",
    )(home, *landed)


def swap(x, axis, size, bits):
    return lax.ppermute(x, axis, [(i, i ^ bits) for i in range(size)])


def swap_late(x, seq, kv, bits):
    pairs = []
    for rank in range(seq):
        for place in range(kv):
            to = (rank ^ bits, place) if 2 * rank >= seq else (rank, place ^ 1)
            pairs.append((rank * kv + place, to[0] * kv + to[1]))
    return lax.ppermute(x, ("seq", "kv"), pairs)


def after(x, *others):
    return lax.optimization_barrier((x, *others))[0]


def make_shards(seq, kv):
    def shards(queries, keys, values, out_weight):
        block = queries.shape[0]
        per_span = SPAN // block
        rank = lax.axis_index("seq").astype(jnp.int32).reshape(1)
        place = lax.axis_index("kv").astype(jnp.int32).reshape(1)
        kinds = min(3, max(2, seq // per_span))
        tables = rope_tables(block)
        by_head = jnp.transpose(queries, (1, 0, 2))
        pieces = {0: prepare(rank, keys[:, 0, :], values[:, 0, :], tables)}

        def send(offset, step, *others):
            pieces[offset] = swap(after(pieces[offset ^ step], *others), "seq", seq, step)

        def pass_on(offset, step, *others):
            source = after(pieces[offset ^ step], *others)
            late = 2 * offset >= seq
            pieces[offset] = swap_late(source, seq, kv, step) if late else swap(source, "seq", seq, step)

        twin_weight = swap(out_weight, "kv", kv, 1)
        for offset in FIRST:
            send(offset, offset)
        rot, *state = begin(
            kinds, rank, place, by_head, tables, out_weight, pieces[0]
        )
        state, staged = state[:3], state[3:]
        for offset in range(2 * per_span, seq, per_span):
            send(offset, offset & -offset)
            for low in range(1, per_span):
                send(offset + low, low)
        calls = CALLS + [list(range(at, at + per_span)) for at in range(2 * per_span, seq, per_span)]

        def blocks(offsets, state, *how):
            return attend(rank, offsets, rot, [pieces[o] for o in offsets], state, *how)

        for offset in LATER:
            pass_on(offset, offset ^ TURN, state[0])
        for offsets, weights in zip(calls[:-1], STAGES + [[]] * len(calls)):
            stage = (place, *[(out_weight, twin_weight)[at] for at in weights]) if weights else ()
            state = blocks(offsets, state, False, 0, block, stage)
            state, staged = state[:3], staged + list(state[3:])
        own, twin, start = [], [], 0
        for rows in ROW_CHUNKS:
            own.append(blocks(calls[-1], state, True, start, rows))
            twin.append(swap(own[-1], "kv", kv, 1))
            start += rows
        landed = []
        for rows in zip(own, twin):
            away = project(
                *rows, *staged, jnp.bfloat16, "away"
            )
            landed.append(swap(away, "kv", kv, 2))
        home = project_home(place, own, twin, out_weight, twin_weight)
        return close(home, landed)

    return shards


def solution(mesh):
    return jax.shard_map(
        make_shards(mesh.shape["seq"], mesh.shape["kv"]),
        mesh=mesh,
        in_specs=(P("seq", "kv", None), P("seq", "kv", None), P("seq", "kv", None), P("kv", None)),
        out_specs=P("seq", "kv"),
        check_vma=False,
    )
```

```python
import functools
import math

import jax
import jax.numpy as jnp
import numpy as np
from jax import lax
from jax.experimental import pallas as pl
from jax.experimental.pallas import tpu as pltpu
from jax.sharding import PartitionSpec as P

HEAD = 128
GROUP = 7
SPAN = 1024
LOCAL = 32
THETA = 10000000.0
NEG = -1e30
SCALE = math.log2(math.e) / math.sqrt(HEAD)
ROW_CHUNKS = (128, 128)
TURN = 6
FIRST = [6, 1, 2, 3]
CALLS = [[1, 2], [3, 6], [5], [4, 7]]
LATER = [5, 4, 7]
STAGES = [[], [1]]
VMEM = pltpu.MemorySpace.VMEM
HBM = pltpu.MemorySpace.HBM
LIMIT = 24 * 2**20
LIGHT = pl.CostEstimate(flops=1, bytes_accessed=1, transcendentals=0)


def rope_tables(block):
    inverse = np.exp(np.arange(HEAD // 2, dtype=np.float64) * (-2.0 * math.log(THETA) / HEAD))
    inner = np.arange(SPAN)
    first = np.minimum(np.arange(block) + SPAN, SPAN + LOCAL)
    far = np.full((block,), SPAN + LOCAL)
    angles = np.concatenate([inner, first, far])[:, None] * inverse
    cosine, sine = np.cos(angles), np.sin(angles)
    return (
        jnp.asarray(np.concatenate([cosine, cosine], 1), jnp.float32),
        jnp.asarray(np.concatenate([-sine, sine], 1), jnp.float32),
    )


def rotated(x, cosine, sine):
    x = x.astype(jnp.float32)
    return x * cosine + pltpu.roll(x, HEAD // 2, 1) * sine


def in_hbm(x):
    return pltpu.with_memory_space_constraint(x, HBM)


def prepare_kernel(rank_ref, key_hbm, value_hbm, cos_hbm, sin_hbm, out_ref, key_ref, cos_ref, sin_ref, sems):
    block = key_ref.shape[0]
    rows = pl.ds(pl.multiple_of(rank_ref[0] % (SPAN // block) * block, block), block)
    copies = [
        pltpu.make_async_copy(key_hbm, key_ref, sems.at[0]),
        pltpu.make_async_copy(cos_hbm.at[rows], cos_ref, sems.at[1]),
        pltpu.make_async_copy(sin_hbm.at[rows], sin_ref, sems.at[2]),
        pltpu.make_async_copy(value_hbm, out_ref.at[pl.ds(block, block)], sems.at[3]),
    ]
    for copy in copies:
        copy.start()
    for copy in copies:
        copy.wait()
    out_ref[:block] = rotated(key_ref[...], cos_ref[...], sin_ref[...]).astype(jnp.bfloat16)


def prepare(rank, keys, values, tables):
    block = keys.shape[0]
    return pl.pallas_call(
        prepare_kernel,
        in_specs=[pl.BlockSpec(memory_space=pltpu.SMEM)] + [pl.BlockSpec(memory_space=HBM)] * 4,
        out_specs=pl.BlockSpec(memory_space=VMEM),
        out_shape=jax.ShapeDtypeStruct((2 * block, HEAD), jnp.bfloat16),
        scratch_shapes=[
            pltpu.VMEM((block, HEAD), jnp.bfloat16),
            pltpu.VMEM((block, HEAD), jnp.float32),
            pltpu.VMEM((block, HEAD), jnp.float32),
            pltpu.SemaphoreType.DMA((4,)),
        ],
        compiler_params=pltpu.CompilerParams(vmem_limit_bytes=LIMIT),
        name="rotate_keys",
    )(rank, *[in_hbm(x) for x in (keys, values, *tables)])


def scores_of(query, pieces):
    block = pieces[0].shape[0] // 2
    return [
        lax.dot_general(
            q, piece[:block], (((1,), (1,)), ((), ())), preferred_element_type=jnp.float32
        )
        for q, piece in zip(query, pieces)
    ]


def absorb(scores, lifts, pieces, old):
    block = pieces[0].shape[0] // 2
    lanes = [slice(at, at + HEAD) for at in range(0, block, HEAD)]
    peak = None
    for score, lift in zip(scores, lifts):
        high = functools.reduce(jnp.maximum, [score[:, lane] for lane in lanes])
        if lift is not None:
            high = high - lift
        peak = high if peak is None else jnp.maximum(peak, high)
    top = jnp.max(peak, axis=1, keepdims=True)
    if old is None:
        top = jnp.broadcast_to(top, peak.shape)
        acc, total = None, None
    else:
        top = jnp.maximum(top, old[0])
        factor = jnp.exp2(old[0] - top)
        acc, total = factor * old[1], factor * old[2]
    ones = jnp.ones((block, HEAD), jnp.bfloat16)
    for score, lift, piece in zip(scores, lifts, pieces):
        base = top if lift is None else top + lift
        weight = jnp.exp2(score - jnp.concatenate([base] * len(lanes), 1)).astype(jnp.bfloat16)
        both = jnp.dot(
            weight, jnp.concatenate([piece[block:], ones], 1), preferred_element_type=jnp.float32
        )
        acc = both[:, :HEAD] if acc is None else acc + both[:, :HEAD]
        total = both[:, HEAD:] if total is None else total + both[:, HEAD:]
    return top, acc, total


def column_copies(place, weight_hbm, into, sems):
    columns = into[0].shape[1]
    copies = []
    for flip, ref in enumerate(into):
        at = pl.ds(pl.multiple_of((place ^ (2 * flip)) * columns, columns), columns)
        copies.append(pltpu.make_async_copy(weight_hbm.at[:, at], ref, sems.at[flip]))
    return copies


def begin_kernel(
    kinds, rank_ref, place_ref, query_hbm, cos_hbm, sin_hbm, weight_hbm, piece_ref,
    rot_ref, top_ref, acc_ref, total_ref, *refs,
):
    away_ref, query_ref, cos_ref, sin_ref, sems, weight_sems = refs
    heads, block, _ = query_ref.shape
    per_span = SPAN // block
    rank, place = rank_ref[0], place_ref[0]
    inner = rank % per_span
    places = [inner, jnp.where(inner == 0, per_span, per_span + 1), per_span + 1][:kinds]
    copies = [pltpu.make_async_copy(query_hbm, query_ref, sems.at[0])]
    for kind, at in enumerate(places):
        rows = pl.ds(pl.multiple_of(at * block, block), block)
        copies.append(pltpu.make_async_copy(cos_hbm.at[rows], cos_ref.at[kind], sems.at[1 + 2 * kind]))
        copies.append(pltpu.make_async_copy(sin_hbm.at[rows], sin_ref.at[kind], sems.at[2 + 2 * kind]))
    for copy in copies:
        copy.start()
    loads = column_copies(place ^ 2, weight_hbm, [away_ref], weight_sems)
    for copy in loads:
        copy.start()
    for copy in copies:
        copy.wait()
    causal = lax.broadcasted_iota(jnp.int32, (block, block), 1) <= lax.broadcasted_iota(
        jnp.int32, (block, block), 0
    )
    def turn(kind):
        for head in range(heads):
            rot_ref[kind, head] = (
                rotated(query_ref[head], cos_ref[kind], sin_ref[kind]) * SCALE
            ).astype(jnp.bfloat16)

    def blank(kind):
        rot_ref[kind] = jnp.zeros(rot_ref.shape[1:], rot_ref.dtype)

    turn(0)
    for kind in range(1, kinds):
        pl.when(rank >= kind * per_span)(functools.partial(turn, kind))
        pl.when(rank < kind * per_span)(functools.partial(blank, kind))
    later = scores_of([rot_ref[0, 0]], [piece_ref])
    for head in range(heads):
        now = later
        if head + 1 < heads:
            later = scores_of([rot_ref[0, head + 1]], [piece_ref])
        now = [jnp.where(causal, now[0], NEG)]
        top_ref[head], acc_ref[head], total_ref[head] = absorb(now, [None], [piece_ref], None)
    for copy in loads:
        copy.wait()


def begin(kinds, rank, place, queries, tables, out_weight, piece):
    heads, block, _ = queries.shape
    depth = out_weight.shape[0]
    smem, hbm, vmem = (pl.BlockSpec(memory_space=space) for space in (pltpu.SMEM, HBM, VMEM))
    return pl.pallas_call(
        functools.partial(begin_kernel, kinds),
        in_specs=[smem, smem, hbm, hbm, hbm, hbm, vmem],
        out_specs=[vmem] * 5,
        out_shape=[
            jax.ShapeDtypeStruct((kinds, heads, block, HEAD), jnp.bfloat16),
            *[jax.ShapeDtypeStruct((heads, block, HEAD), jnp.float32)] * 3,
            jax.ShapeDtypeStruct((depth, depth), jnp.bfloat16),
        ],
        scratch_shapes=[
            pltpu.VMEM((heads, block, HEAD), jnp.bfloat16),
            pltpu.VMEM((kinds, block, HEAD), jnp.float32),
            pltpu.VMEM((kinds, block, HEAD), jnp.float32),
            pltpu.SemaphoreType.DMA((1 + 2 * kinds,)),
            pltpu.SemaphoreType.DMA((1,)),
        ],
        cost_estimate=LIGHT,
        compiler_params=pltpu.CompilerParams(vmem_limit_bytes=LIMIT),
        name="attend_0",
    )(rank, place, *[in_hbm(x) for x in (queries, *tables, out_weight)], piece)


def attend_kernel(offsets, kinds, first, last, start, rows, stages, rank_ref, rot_ref, *refs):
    pieces, refs = refs[: len(offsets)], refs[len(offsets) :]
    old, refs = ([], refs) if first else (refs[:3], refs[3:])
    loads = []
    if stages:
        place_ref, *refs, sems = refs
        weights, refs, staged = refs[:stages], refs[stages:-stages], refs[-stages:]
        for at, (weight_hbm, ref) in enumerate(zip(weights, staged)):
            loads += column_copies(place_ref[0] ^ 2, weight_hbm, [ref], sems.at[pl.ds(at, 1)])
    for copy in loads:
        copy.start()
    block = pieces[0].shape[0] // 2
    per_span = SPAN // block
    rank = rank_ref[0]
    lifts = [
        jnp.where((rank ^ offset) <= rank, 0.0, -NEG).astype(jnp.float32) if offset else None
        for offset in offsets
    ]
    picked = []
    for offset in offsets:
        kind = min(offset // per_span, 1)
        if kind and kinds > 2:
            back = rank // per_span - (rank ^ offset) // per_span
            kind = jnp.clip(back, 1, kinds - 1)
        picked.append(kind)
    here = slice(start, start + rows)
    if 0 in offsets:
        causal = lax.broadcasted_iota(jnp.int32, (rows, block), 1) <= start + lax.broadcasted_iota(
            jnp.int32, (rows, block), 0
        )

    def scores_at(head):
        scores = scores_of([rot_ref[kind, head, here] for kind in picked], pieces)
        return [
            score if offset else jnp.where(causal, score, NEG)
            for offset, score in zip(offsets, scores)
        ]

    def put(head, top, acc, total):
        if last:
            refs[0][:, head * HEAD : (head + 1) * HEAD] = (acc / total).astype(jnp.bfloat16)
        else:
            refs[0][head], refs[1][head], refs[2][head] = top, acc, total

    def meet():
        later = scores_at(0)
        for head in range(GROUP):
            now = later
            if head + 1 < GROUP:
                later = scores_at(head + 1)
            put(
                head,
                *absorb(now, lifts, pieces, [ref[head, here] for ref in old] or None),
            )

    def keep():
        for head in range(GROUP):
            put(head, *[ref[head, here] for ref in old])

    if first:
        meet()
    else:
        seen = functools.reduce(jnp.logical_or, [(rank ^ offset) <= rank for offset in offsets])
        pl.when(seen)(meet)
        pl.when(jnp.logical_not(seen))(keep)
    for copy in loads:
        copy.wait()


def attend(rank, offsets, rot, pieces, state, last, start, rows, stage=()):
    block = pieces[0].shape[0] // 2
    smem, vmem = (pl.BlockSpec(memory_space=space) for space in (pltpu.SMEM, VMEM))
    if last:
        out_specs = vmem
        out_shape = jax.ShapeDtypeStruct((rows, GROUP * HEAD), jnp.bfloat16)
    else:
        out_specs = [vmem] * 3
        out_shape = [jax.ShapeDtypeStruct((GROUP, rows, HEAD), jnp.float32)] * 3
    args, in_specs, scratch = [], [], []
    if stage:
        place, *weights = stage
        depth = weights[0].shape[0]
        args = [place, *[in_hbm(weight) for weight in weights]]
        in_specs = [smem] + [pl.BlockSpec(memory_space=HBM)] * len(weights)
        out_specs = [*out_specs, *[vmem] * len(weights)]
        out_shape = [
            *out_shape,
            *[jax.ShapeDtypeStruct((depth, depth), jnp.bfloat16)] * len(weights),
        ]
        scratch = [pltpu.SemaphoreType.DMA((len(weights),))]
    return pl.pallas_call(
        functools.partial(
            attend_kernel,
            tuple(offsets),
            rot.shape[0],
            not state,
            last,
            start,
            rows,
            len(stage[1:]),
        ),
        in_specs=[smem] + [vmem] * (1 + len(pieces) + len(state)) + in_specs,
        scratch_shapes=scratch,
        out_specs=out_specs,
        out_shape=out_shape,
        cost_estimate=LIGHT,
        compiler_params=pltpu.CompilerParams(vmem_limit_bytes=LIMIT),
        name="attend_" + "_".join(map(str, offsets)),
    )(rank, rot, *pieces, *state, *args)


def project_kernel(own_ref, twin_ref, own_weight, twin_weight, out_ref):
    out_ref[...] = (
        jnp.dot(own_ref[...], own_weight[...], preferred_element_type=jnp.float32)
        + jnp.dot(twin_ref[...], twin_weight[...], preferred_element_type=jnp.float32)
    ).astype(out_ref.dtype)


def project(own, twin, own_weight, twin_weight, dtype, name):
    vmem = pl.BlockSpec(memory_space=VMEM)
    return pl.pallas_call(
        project_kernel,
        in_specs=[vmem] * 4,
        out_specs=vmem,
        out_shape=jax.ShapeDtypeStruct((own.shape[0], own_weight.shape[1]), dtype),
        cost_estimate=LIGHT,
        compiler_params=pltpu.CompilerParams(vmem_limit_bytes=LIMIT),
        name=name,
    )(own, twin, own_weight, twin_weight)


def home_kernel(count, place_ref, own_hbm, twin_hbm, *refs):
    own_refs, twin_refs, refs = refs[:count], refs[count : 2 * count], refs[2 * count :]
    out_ref, own_weight, twin_weight, sems = refs
    loads = []
    for at, (hbm, ref) in enumerate(((own_hbm, own_weight), (twin_hbm, twin_weight))):
        loads += column_copies(place_ref[0], hbm, [ref], sems.at[pl.ds(at, 1)])
    for load in loads:
        load.start()
    for load in loads:
        load.wait()
    start = 0
    for own, twin in zip(own_refs, twin_refs):
        rows = pl.ds(start, own.shape[0])
        out_ref[rows] = jnp.dot(
            own[...], own_weight[...], preferred_element_type=jnp.float32
        ) + jnp.dot(twin[...], twin_weight[...], preferred_element_type=jnp.float32)
        start += own.shape[0]


def project_home(place, own, twin, own_weight, twin_weight):
    smem, hbm, vmem = (pl.BlockSpec(memory_space=space) for space in (pltpu.SMEM, HBM, VMEM))
    rows = sum(x.shape[0] for x in own)
    depth = own_weight.shape[0]
    return pl.pallas_call(
        functools.partial(home_kernel, len(own)),
        in_specs=[smem, hbm, hbm] + [vmem] * (2 * len(own)),
        out_specs=vmem,
        out_shape=jax.ShapeDtypeStruct((rows, depth), jnp.float32),
        scratch_shapes=[
            pltpu.VMEM((depth, depth), jnp.bfloat16),
            pltpu.VMEM((depth, depth), jnp.bfloat16),
            pltpu.SemaphoreType.DMA((2,)),
        ],
        cost_estimate=LIGHT,
        compiler_params=pltpu.CompilerParams(vmem_limit_bytes=LIMIT),
        name="home",
    )(place, in_hbm(own_weight), in_hbm(twin_weight), *own, *twin)


def close_kernel(home_ref, *refs):
    *landed_refs, out_hbm, sum_ref, sems = refs
    copies, start = [], 0
    for at, landed in enumerate(landed_refs):
        rows = pl.ds(start, landed.shape[0])
        sum_ref[rows] = (home_ref[rows] + landed[...].astype(jnp.float32)).astype(sum_ref.dtype)
        copies.append(pltpu.make_async_copy(sum_ref.at[rows], out_hbm.at[rows], sems.at[at]))
        copies[-1].start()
        start += landed.shape[0]
    for copy in copies:
        copy.wait()


def close(home, landed):
    vmem, hbm = (pl.BlockSpec(memory_space=space) for space in (VMEM, HBM))
    return pl.pallas_call(
        close_kernel,
        in_specs=[vmem] * (1 + len(landed)),
        out_specs=hbm,
        out_shape=jax.ShapeDtypeStruct(home.shape, jnp.bfloat16),
        scratch_shapes=[
            pltpu.VMEM(home.shape, jnp.bfloat16),
            pltpu.SemaphoreType.DMA((len(landed),)),
        ],
        cost_estimate=LIGHT,
        compiler_params=pltpu.CompilerParams(vmem_limit_bytes=LIMIT),
        name="close",
    )(home, *landed)


def swap(x, axis, size, bits):
    return lax.ppermute(x, axis, [(i, i ^ bits) for i in range(size)])


def swap_late(x, seq, kv, bits):
    pairs = []
    for rank in range(seq):
        for place in range(kv):
            to = (rank ^ bits, place) if 2 * rank >= seq else (rank, place ^ 1)
            pairs.append((rank * kv + place, to[0] * kv + to[1]))
    return lax.ppermute(x, ("seq", "kv"), pairs)


def after(x, *others):
    return lax.optimization_barrier((x, *others))[0]


def make_shards(seq, kv):
    def shards(queries, keys, values, out_weight):
        block = queries.shape[0]
        per_span = SPAN // block
        rank = lax.axis_index("seq").astype(jnp.int32).reshape(1)
        place = lax.axis_index("kv").astype(jnp.int32).reshape(1)
        kinds = min(3, max(2, seq // per_span))
        tables = rope_tables(block)
        by_head = jnp.transpose(queries, (1, 0, 2))
        pieces = {0: prepare(rank, keys[:, 0, :], values[:, 0, :], tables)}

        def send(offset, step, *others):
            pieces[offset] = swap(after(pieces[offset ^ step], *others), "seq", seq, step)

        def pass_on(offset, step, *others):
            source = after(pieces[offset ^ step], *others)
            late = 2 * offset >= seq
            pieces[offset] = swap_late(source, seq, kv, step) if late else swap(source, "seq", seq, step)

        twin_weight = swap(out_weight, "kv", kv, 1)
        for offset in FIRST:
            send(offset, offset)
        rot, *state = begin(
            kinds, rank, place, by_head, tables, out_weight, pieces[0]
        )
        state, staged = state[:3], state[3:]
        for offset in range(2 * per_span, seq, per_span):
            send(offset, offset & -offset)
            for low in range(1, per_span):
                send(offset + low, low)
        calls = CALLS + [list(range(at, at + per_span)) for at in range(2 * per_span, seq, per_span)]

        def blocks(offsets, state, *how):
            return attend(rank, offsets, rot, [pieces[o] for o in offsets], state, *how)

        for offset in LATER:
            pass_on(offset, offset ^ TURN, state[0])
        for offsets, weights in zip(calls[:-1], STAGES + [[]] * len(calls)):
            stage = (place, *[(out_weight, twin_weight)[at] for at in weights]) if weights else ()
            state = blocks(offsets, state, False, 0, block, stage)
            state, staged = state[:3], staged + list(state[3:])
        own, twin, start = [], [], 0
        for rows in ROW_CHUNKS:
            own.append(blocks(calls[-1], state, True, start, rows))
            twin.append(swap(own[-1], "kv", kv, 1))
            start += rows
        landed = []
        for rows in zip(own, twin):
            away = project(
                *rows, *staged, jnp.bfloat16, "away"
            )
            landed.append(swap(away, "kv", kv, 2))
        home = project_home(place, own, twin, out_weight, twin_weight)
        return close(home, landed)

    return shards


def solution(mesh):
    return jax.shard_map(
        make_shards(mesh.shape["seq"], mesh.shape["kv"]),
        mesh=mesh,
        in_specs=(P("seq", "kv", None), P("seq", "kv", None), P("seq", "kv", None), P("kv", None)),
        out_specs=P("seq", "kv"),
        check_vma=False,
    )
```

```python
import functools
import math

import jax
import jax.numpy as jnp
import numpy as np
from jax import lax
from jax.experimental import pallas as pl
from jax.experimental.pallas import tpu as pltpu
from jax.sharding import PartitionSpec as P

HEAD = 128
GROUP = 7
SPAN = 1024
LOCAL = 32
THETA = 10000000.0
NEG = -1e30
SCALE = math.log2(math.e) / math.sqrt(HEAD)
ROW_CHUNKS = (128, 128)
TURN = 6
FIRST = [6, 1, 2, 3]
CALLS = [[1, 2], [3, 6], [5], [4, 7]]
LATER = [5, 4, 7]
STAGES = [[], [1]]
VMEM = pltpu.MemorySpace.VMEM
HBM = pltpu.MemorySpace.HBM
LIMIT = 24 * 2**20
LIGHT = pl.CostEstimate(flops=1, bytes_accessed=1, transcendentals=0)


def rope_tables(block):
    inverse = np.exp(np.arange(HEAD // 2, dtype=np.float64) * (-2.0 * math.log(THETA) / HEAD))
    inner = np.arange(SPAN)
    first = np.minimum(np.arange(block) + SPAN, SPAN + LOCAL)
    far = np.full((block,), SPAN + LOCAL)
    angles = np.concatenate([inner, first, far])[:, None] * inverse
    cosine, sine = np.cos(angles), np.sin(angles)
    return (
        jnp.asarray(np.concatenate([cosine, cosine], 1), jnp.float32),
        jnp.asarray(np.concatenate([-sine, sine], 1), jnp.float32),
    )


def rotated(x, cosine, sine):
    x = x.astype(jnp.float32)
    return x * cosine + pltpu.roll(x, HEAD // 2, 1) * sine


def in_hbm(x):
    return pltpu.with_memory_space_constraint(x, HBM)


def prepare_kernel(rank_ref, key_hbm, value_hbm, cos_hbm, sin_hbm, out_ref, key_ref, cos_ref, sin_ref, sems):
    block = key_ref.shape[0]
    rows = pl.ds(pl.multiple_of(rank_ref[0] % (SPAN // block) * block, block), block)
    copies = [
        pltpu.make_async_copy(key_hbm, key_ref, sems.at[0]),
        pltpu.make_async_copy(cos_hbm.at[rows], cos_ref, sems.at[1]),
        pltpu.make_async_copy(sin_hbm.at[rows], sin_ref, sems.at[2]),
        pltpu.make_async_copy(value_hbm, out_ref.at[pl.ds(block, block)], sems.at[3]),
    ]
    for copy in copies:
        copy.start()
    for copy in copies:
        copy.wait()
    out_ref[:block] = rotated(key_ref[...], cos_ref[...], sin_ref[...]).astype(jnp.bfloat16)


def prepare(rank, keys, values, tables):
    block = keys.shape[0]
    return pl.pallas_call(
        prepare_kernel,
        in_specs=[pl.BlockSpec(memory_space=pltpu.SMEM)] + [pl.BlockSpec(memory_space=HBM)] * 4,
        out_specs=pl.BlockSpec(memory_space=VMEM),
        out_shape=jax.ShapeDtypeStruct((2 * block, HEAD), jnp.bfloat16),
        scratch_shapes=[
            pltpu.VMEM((block, HEAD), jnp.bfloat16),
            pltpu.VMEM((block, HEAD), jnp.float32),
            pltpu.VMEM((block, HEAD), jnp.float32),
            pltpu.SemaphoreType.DMA((4,)),
        ],
        compiler_params=pltpu.CompilerParams(vmem_limit_bytes=LIMIT),
        name="rotate_keys",
    )(rank, *[in_hbm(x) for x in (keys, values, *tables)])


def scores_of(query, pieces):
    block = pieces[0].shape[0] // 2
    return [
        lax.dot_general(
            q, piece[:block], (((1,), (1,)), ((), ())), preferred_element_type=jnp.float32
        )
        for q, piece in zip(query, pieces)
    ]


def absorb(scores, lifts, pieces, old):
    block = pieces[0].shape[0] // 2
    lanes = [slice(at, at + HEAD) for at in range(0, block, HEAD)]
    peak = None
    for score, lift in zip(scores, lifts):
        high = functools.reduce(jnp.maximum, [score[:, lane] for lane in lanes])
        if lift is not None:
            high = high - lift
        peak = high if peak is None else jnp.maximum(peak, high)
    top = jnp.max(peak, axis=1, keepdims=True)
    if old is None:
        top = jnp.broadcast_to(top, peak.shape)
        acc, total = None, None
    else:
        top = jnp.maximum(top, old[0])
        factor = jnp.exp2((old[0] - top) * SCALE)
        acc, total = factor * old[1], factor * old[2]
    ones = jnp.ones((block, HEAD), jnp.bfloat16)
    for score, lift, piece in zip(scores, lifts, pieces):
        base = top if lift is None else top + lift
        weight = jnp.exp2((score - jnp.concatenate([base] * len(lanes), 1)) * SCALE).astype(jnp.bfloat16)
        both = jnp.dot(
            weight, jnp.concatenate([piece[block:], ones], 1), preferred_element_type=jnp.float32
        )
        acc = both[:, :HEAD] if acc is None else acc + both[:, :HEAD]
        total = both[:, HEAD:] if total is None else total + both[:, HEAD:]
    return top, acc, total


def column_copies(place, weight_hbm, into, sems):
    columns = into[0].shape[1]
    copies = []
    for flip, ref in enumerate(into):
        at = pl.ds(pl.multiple_of((place ^ (2 * flip)) * columns, columns), columns)
        copies.append(pltpu.make_async_copy(weight_hbm.at[:, at], ref, sems.at[flip]))
    return copies


def begin_kernel(
    kinds, rank_ref, place_ref, query_hbm, cos_hbm, sin_hbm, weight_hbm, piece_ref,
    rot_ref, top_ref, acc_ref, total_ref, *refs,
):
    away_ref, query_ref, cos_ref, sin_ref, sems, weight_sems = refs
    heads, block, _ = query_ref.shape
    per_span = SPAN // block
    rank, place = rank_ref[0], place_ref[0]
    inner = rank % per_span
    places = [inner, jnp.where(inner == 0, per_span, per_span + 1), per_span + 1][:kinds]
    copies = [pltpu.make_async_copy(query_hbm, query_ref, sems.at[0])]
    for kind, at in enumerate(places):
        rows = pl.ds(pl.multiple_of(at * block, block), block)
        copies.append(pltpu.make_async_copy(cos_hbm.at[rows], cos_ref.at[kind], sems.at[1 + 2 * kind]))
        copies.append(pltpu.make_async_copy(sin_hbm.at[rows], sin_ref.at[kind], sems.at[2 + 2 * kind]))
    for copy in copies:
        copy.start()
    loads = column_copies(place ^ 2, weight_hbm, [away_ref], weight_sems)
    for copy in loads:
        copy.start()
    for copy in copies:
        copy.wait()
    causal = lax.broadcasted_iota(jnp.int32, (block, block), 1) <= lax.broadcasted_iota(
        jnp.int32, (block, block), 0
    )
    def turn(kind):
        for head in range(heads):
            rot_ref[kind, head] = rotated(query_ref[head], cos_ref[kind], sin_ref[kind]).astype(
                jnp.bfloat16
            )

    def blank(kind):
        rot_ref[kind] = jnp.zeros(rot_ref.shape[1:], rot_ref.dtype)

    turn(0)
    for kind in range(1, kinds):
        pl.when(rank >= kind * per_span)(functools.partial(turn, kind))
        pl.when(rank < kind * per_span)(functools.partial(blank, kind))
    later = scores_of([rot_ref[0, 0]], [piece_ref])
    for head in range(heads):
        now = later
        if head + 1 < heads:
            later = scores_of([rot_ref[0, head + 1]], [piece_ref])
        now = [jnp.where(causal, now[0], NEG)]
        top_ref[head], acc_ref[head], total_ref[head] = absorb(now, [None], [piece_ref], None)
    for copy in loads:
        copy.wait()


def begin(kinds, rank, place, queries, tables, out_weight, piece):
    heads, block, _ = queries.shape
    depth = out_weight.shape[0]
    smem, hbm, vmem = (pl.BlockSpec(memory_space=space) for space in (pltpu.SMEM, HBM, VMEM))
    return pl.pallas_call(
        functools.partial(begin_kernel, kinds),
        in_specs=[smem, smem, hbm, hbm, hbm, hbm, vmem],
        out_specs=[vmem] * 5,
        out_shape=[
            jax.ShapeDtypeStruct((kinds, heads, block, HEAD), jnp.bfloat16),
            *[jax.ShapeDtypeStruct((heads, block, HEAD), jnp.float32)] * 3,
            jax.ShapeDtypeStruct((depth, depth), jnp.bfloat16),
        ],
        scratch_shapes=[
            pltpu.VMEM((heads, block, HEAD), jnp.bfloat16),
            pltpu.VMEM((kinds, block, HEAD), jnp.float32),
            pltpu.VMEM((kinds, block, HEAD), jnp.float32),
            pltpu.SemaphoreType.DMA((1 + 2 * kinds,)),
            pltpu.SemaphoreType.DMA((1,)),
        ],
        cost_estimate=LIGHT,
        compiler_params=pltpu.CompilerParams(vmem_limit_bytes=LIMIT),
        name="attend_0",
    )(rank, place, *[in_hbm(x) for x in (queries, *tables, out_weight)], piece)


def attend_kernel(offsets, kinds, first, last, start, rows, stages, rank_ref, rot_ref, *refs):
    pieces, refs = refs[: len(offsets)], refs[len(offsets) :]
    old, refs = ([], refs) if first else (refs[:3], refs[3:])
    loads = []
    if stages:
        place_ref, *refs, sems = refs
        weights, refs, staged = refs[:stages], refs[stages:-stages], refs[-stages:]
        for at, (weight_hbm, ref) in enumerate(zip(weights, staged)):
            loads += column_copies(place_ref[0] ^ 2, weight_hbm, [ref], sems.at[pl.ds(at, 1)])
    for copy in loads:
        copy.start()
    block = pieces[0].shape[0] // 2
    per_span = SPAN // block
    rank = rank_ref[0]
    lifts = [
        jnp.where((rank ^ offset) <= rank, 0.0, -NEG).astype(jnp.float32) if offset else None
        for offset in offsets
    ]
    picked = []
    for offset in offsets:
        kind = min(offset // per_span, 1)
        if kind and kinds > 2:
            back = rank // per_span - (rank ^ offset) // per_span
            kind = jnp.clip(back, 1, kinds - 1)
        picked.append(kind)
    here = slice(start, start + rows)
    if 0 in offsets:
        causal = lax.broadcasted_iota(jnp.int32, (rows, block), 1) <= start + lax.broadcasted_iota(
            jnp.int32, (rows, block), 0
        )

    def scores_at(head):
        scores = scores_of([rot_ref[kind, head, here] for kind in picked], pieces)
        return [
            score if offset else jnp.where(causal, score, NEG)
            for offset, score in zip(offsets, scores)
        ]

    def put(head, top, acc, total):
        if last:
            refs[0][:, head * HEAD : (head + 1) * HEAD] = (acc / total).astype(jnp.bfloat16)
        else:
            refs[0][head], refs[1][head], refs[2][head] = top, acc, total

    def meet():
        later = scores_at(0)
        for head in range(GROUP):
            now = later
            if head + 1 < GROUP:
                later = scores_at(head + 1)
            put(
                head,
                *absorb(now, lifts, pieces, [ref[head, here] for ref in old] or None),
            )

    def keep():
        for head in range(GROUP):
            put(head, *[ref[head, here] for ref in old])

    if first:
        meet()
    else:
        seen = functools.reduce(jnp.logical_or, [(rank ^ offset) <= rank for offset in offsets])
        pl.when(seen)(meet)
        pl.when(jnp.logical_not(seen))(keep)
    for copy in loads:
        copy.wait()


def attend(rank, offsets, rot, pieces, state, last, start, rows, stage=()):
    block = pieces[0].shape[0] // 2
    smem, vmem = (pl.BlockSpec(memory_space=space) for space in (pltpu.SMEM, VMEM))
    if last:
        out_specs = vmem
        out_shape = jax.ShapeDtypeStruct((rows, GROUP * HEAD), jnp.bfloat16)
    else:
        out_specs = [vmem] * 3
        out_shape = [jax.ShapeDtypeStruct((GROUP, rows, HEAD), jnp.float32)] * 3
    args, in_specs, scratch = [], [], []
    if stage:
        place, *weights = stage
        depth = weights[0].shape[0]
        args = [place, *[in_hbm(weight) for weight in weights]]
        in_specs = [smem] + [pl.BlockSpec(memory_space=HBM)] * len(weights)
        out_specs = [*out_specs, *[vmem] * len(weights)]
        out_shape = [
            *out_shape,
            *[jax.ShapeDtypeStruct((depth, depth), jnp.bfloat16)] * len(weights),
        ]
        scratch = [pltpu.SemaphoreType.DMA((len(weights),))]
    return pl.pallas_call(
        functools.partial(
            attend_kernel,
            tuple(offsets),
            rot.shape[0],
            not state,
            last,
            start,
            rows,
            len(stage[1:]),
        ),
        in_specs=[smem] + [vmem] * (1 + len(pieces) + len(state)) + in_specs,
        scratch_shapes=scratch,
        out_specs=out_specs,
        out_shape=out_shape,
        cost_estimate=LIGHT,
        compiler_params=pltpu.CompilerParams(vmem_limit_bytes=LIMIT),
        name="attend_" + "_".join(map(str, offsets)),
    )(rank, rot, *pieces, *state, *args)


def project_kernel(own_ref, twin_ref, own_weight, twin_weight, out_ref):
    out_ref[...] = (
        jnp.dot(own_ref[...], own_weight[...], preferred_element_type=jnp.float32)
        + jnp.dot(twin_ref[...], twin_weight[...], preferred_element_type=jnp.float32)
    ).astype(out_ref.dtype)


def project(own, twin, own_weight, twin_weight, dtype, name):
    vmem = pl.BlockSpec(memory_space=VMEM)
    return pl.pallas_call(
        project_kernel,
        in_specs=[vmem] * 4,
        out_specs=vmem,
        out_shape=jax.ShapeDtypeStruct((own.shape[0], own_weight.shape[1]), dtype),
        cost_estimate=LIGHT,
        compiler_params=pltpu.CompilerParams(vmem_limit_bytes=LIMIT),
        name=name,
    )(own, twin, own_weight, twin_weight)


def home_kernel(count, place_ref, own_hbm, twin_hbm, *refs):
    own_refs, twin_refs, refs = refs[:count], refs[count : 2 * count], refs[2 * count :]
    out_ref, own_weight, twin_weight, sems = refs
    loads = []
    for at, (hbm, ref) in enumerate(((own_hbm, own_weight), (twin_hbm, twin_weight))):
        loads += column_copies(place_ref[0], hbm, [ref], sems.at[pl.ds(at, 1)])
    for load in loads:
        load.start()
    for load in loads:
        load.wait()
    start = 0
    for own, twin in zip(own_refs, twin_refs):
        rows = pl.ds(start, own.shape[0])
        out_ref[rows] = jnp.dot(
            own[...], own_weight[...], preferred_element_type=jnp.float32
        ) + jnp.dot(twin[...], twin_weight[...], preferred_element_type=jnp.float32)
        start += own.shape[0]


def project_home(place, own, twin, own_weight, twin_weight):
    smem, hbm, vmem = (pl.BlockSpec(memory_space=space) for space in (pltpu.SMEM, HBM, VMEM))
    rows = sum(x.shape[0] for x in own)
    depth = own_weight.shape[0]
    return pl.pallas_call(
        functools.partial(home_kernel, len(own)),
        in_specs=[smem, hbm, hbm] + [vmem] * (2 * len(own)),
        out_specs=vmem,
        out_shape=jax.ShapeDtypeStruct((rows, depth), jnp.float32),
        scratch_shapes=[
            pltpu.VMEM((depth, depth), jnp.bfloat16),
            pltpu.VMEM((depth, depth), jnp.bfloat16),
            pltpu.SemaphoreType.DMA((2,)),
        ],
        cost_estimate=LIGHT,
        compiler_params=pltpu.CompilerParams(vmem_limit_bytes=LIMIT),
        name="home",
    )(place, in_hbm(own_weight), in_hbm(twin_weight), *own, *twin)


def close_kernel(home_ref, *refs):
    *landed_refs, out_hbm, sum_ref, sems = refs
    copies, start = [], 0
    for at, landed in enumerate(landed_refs):
        rows = pl.ds(start, landed.shape[0])
        sum_ref[rows] = (home_ref[rows] + landed[...].astype(jnp.float32)).astype(sum_ref.dtype)
        copies.append(pltpu.make_async_copy(sum_ref.at[rows], out_hbm.at[rows], sems.at[at]))
        copies[-1].start()
        start += landed.shape[0]
    for copy in copies:
        copy.wait()


def close(home, landed):
    vmem, hbm = (pl.BlockSpec(memory_space=space) for space in (VMEM, HBM))
    return pl.pallas_call(
        close_kernel,
        in_specs=[vmem] * (1 + len(landed)),
        out_specs=hbm,
        out_shape=jax.ShapeDtypeStruct(home.shape, jnp.bfloat16),
        scratch_shapes=[
            pltpu.VMEM(home.shape, jnp.bfloat16),
            pltpu.SemaphoreType.DMA((len(landed),)),
        ],
        cost_estimate=LIGHT,
        compiler_params=pltpu.CompilerParams(vmem_limit_bytes=LIMIT),
        name="close",
    )(home, *landed)


def swap(x, axis, size, bits):
    return lax.ppermute(x, axis, [(i, i ^ bits) for i in range(size)])


def swap_late(x, seq, kv, bits):
    pairs = []
    for rank in range(seq):
        for place in range(kv):
            to = (rank ^ bits, place) if 2 * rank >= seq else (rank, place ^ 1)
            pairs.append((rank * kv + place, to[0] * kv + to[1]))
    return lax.ppermute(x, ("seq", "kv"), pairs)


def after(x, *others):
    return lax.optimization_barrier((x, *others))[0]


def make_shards(seq, kv):
    def shards(queries, keys, values, out_weight):
        block = queries.shape[0]
        per_span = SPAN // block
        rank = lax.axis_index("seq").astype(jnp.int32).reshape(1)
        place = lax.axis_index("kv").astype(jnp.int32).reshape(1)
        kinds = min(3, max(2, seq // per_span))
        tables = rope_tables(block)
        by_head = jnp.transpose(queries, (1, 0, 2))
        pieces = {0: prepare(rank, keys[:, 0, :], values[:, 0, :], tables)}

        def send(offset, step, *others):
            pieces[offset] = swap(after(pieces[offset ^ step], *others), "seq", seq, step)

        def pass_on(offset, step, *others):
            source = after(pieces[offset ^ step], *others)
            late = 2 * offset >= seq
            pieces[offset] = swap_late(source, seq, kv, step) if late else swap(source, "seq", seq, step)

        twin_weight = swap(out_weight, "kv", kv, 1)
        for offset in FIRST:
            send(offset, offset)
        rot, *state = begin(
            kinds, rank, place, by_head, tables, out_weight, pieces[0]
        )
        state, staged = state[:3], state[3:]
        for offset in range(2 * per_span, seq, per_span):
            send(offset, offset & -offset)
            for low in range(1, per_span):
                send(offset + low, low)
        calls = CALLS + [list(range(at, at + per_span)) for at in range(2 * per_span, seq, per_span)]

        def blocks(offsets, state, *how):
            return attend(rank, offsets, rot, [pieces[o] for o in offsets], state, *how)

        for offset in LATER:
            pass_on(offset, offset ^ TURN, state[0])
        for offsets, weights in zip(calls[:-1], STAGES + [[]] * len(calls)):
            stage = (place, *[(out_weight, twin_weight)[at] for at in weights]) if weights else ()
            state = blocks(offsets, state, False, 0, block, stage)
            state, staged = state[:3], staged + list(state[3:])
        own, twin, start = [], [], 0
        for rows in ROW_CHUNKS:
            own.append(blocks(calls[-1], state, True, start, rows))
            twin.append(swap(own[-1], "kv", kv, 1))
            start += rows
        landed = []
        for rows in zip(own, twin):
            away = project(
                *rows, *staged, jnp.bfloat16, "away"
            )
            landed.append(swap(away, "kv", kv, 2))
        home = project_home(place, own, twin, out_weight, twin_weight)
        return close(home, landed)

    return shards


def solution(mesh):
    return jax.shard_map(
        make_shards(mesh.shape["seq"], mesh.shape["kv"]),
        mesh=mesh,
        in_specs=(P("seq", "kv", None), P("seq", "kv", None), P("seq", "kv", None), P("kv", None)),
        out_specs=P("seq", "kv"),
        check_vma=False,
    )
```

```python
import functools
import math

import jax
import jax.numpy as jnp
import numpy as np
from jax import lax
from jax.experimental import pallas as pl
from jax.experimental.pallas import tpu as pltpu
from jax.sharding import PartitionSpec as P

HEAD = 128
GROUP = 7
SPAN = 1024
LOCAL = 32
THETA = 10000000.0
NEG = -1e30
SCALE = math.log2(math.e) / math.sqrt(HEAD)
ROW_CHUNKS = (128, 128)
TURN = 6
FIRST = [6, 1, 2, 3]
CALLS = [[1, 2], [3, 6], [5], [4, 7]]
LATER = [5, 4, 7]
STAGES = [[], [1]]
VMEM = pltpu.MemorySpace.VMEM
HBM = pltpu.MemorySpace.HBM
LIMIT = 24 * 2**20
LIGHT = pl.CostEstimate(flops=1, bytes_accessed=1, transcendentals=0)


def rope_tables(block):
    inverse = np.exp(np.arange(HEAD // 2, dtype=np.float64) * (-2.0 * math.log(THETA) / HEAD))
    inner = np.arange(SPAN)
    first = np.minimum(np.arange(block) + SPAN, SPAN + LOCAL)
    far = np.full((block,), SPAN + LOCAL)
    angles = np.concatenate([inner, first, far])[:, None] * inverse
    cosine, sine = np.cos(angles), np.sin(angles)
    return (
        jnp.asarray(np.concatenate([cosine, cosine], 1), jnp.float32),
        jnp.asarray(np.concatenate([-sine, sine], 1), jnp.float32),
    )


def rotated(x, cosine, sine):
    x = x.astype(jnp.float32)
    return x * cosine + pltpu.roll(x, HEAD // 2, 1) * sine


def in_hbm(x):
    return pltpu.with_memory_space_constraint(x, HBM)


def prepare_kernel(rank_ref, key_hbm, value_hbm, cos_hbm, sin_hbm, out_ref, key_ref, cos_ref, sin_ref, sems):
    block = key_ref.shape[0]
    rows = pl.ds(pl.multiple_of(rank_ref[0] % (SPAN // block) * block, block), block)
    copies = [
        pltpu.make_async_copy(key_hbm, key_ref, sems.at[0]),
        pltpu.make_async_copy(cos_hbm.at[rows], cos_ref, sems.at[1]),
        pltpu.make_async_copy(sin_hbm.at[rows], sin_ref, sems.at[2]),
        pltpu.make_async_copy(value_hbm, out_ref.at[pl.ds(block, block)], sems.at[3]),
    ]
    for copy in copies:
        copy.start()
    for copy in copies:
        copy.wait()
    out_ref[:block] = rotated(key_ref[...], cos_ref[...], sin_ref[...]).astype(jnp.bfloat16)


def prepare(rank, keys, values, tables):
    block = keys.shape[0]
    return pl.pallas_call(
        prepare_kernel,
        in_specs=[pl.BlockSpec(memory_space=pltpu.SMEM)] + [pl.BlockSpec(memory_space=HBM)] * 4,
        out_specs=pl.BlockSpec(memory_space=VMEM),
        out_shape=jax.ShapeDtypeStruct((2 * block, HEAD), jnp.bfloat16),
        scratch_shapes=[
            pltpu.VMEM((block, HEAD), jnp.bfloat16),
            pltpu.VMEM((block, HEAD), jnp.float32),
            pltpu.VMEM((block, HEAD), jnp.float32),
            pltpu.SemaphoreType.DMA((4,)),
        ],
        compiler_params=pltpu.CompilerParams(vmem_limit_bytes=LIMIT),
        name="rotate_keys",
    )(rank, *[in_hbm(x) for x in (keys, values, *tables)])


def scores_of(query, pieces):
    block = pieces[0].shape[0] // 2
    return [
        lax.dot_general(
            q, piece[:block], (((1,), (1,)), ((), ())), preferred_element_type=jnp.float32
        )
        for q, piece in zip(query, pieces)
    ]


def absorb(scores, lifts, pieces, old):
    block = pieces[0].shape[0] // 2
    lanes = [slice(at, at + HEAD) for at in range(0, block, HEAD)]
    peak = None
    for score, lift in zip(scores, lifts):
        high = functools.reduce(jnp.maximum, [score[:, lane] for lane in lanes])
        if lift is not None:
            high = high - lift
        peak = high if peak is None else jnp.maximum(peak, high)
    top = jnp.max(peak, axis=1, keepdims=True)
    if old is None:
        top = jnp.broadcast_to(top, peak.shape)
        acc, total = None, None
    else:
        top = jnp.maximum(top, old[0])
        factor = jnp.exp2((old[0] - top) * SCALE)
        acc, total = factor * old[1], factor * old[2]
    ones = jnp.ones((block, HEAD), jnp.bfloat16)
    for score, lift, piece in zip(scores, lifts, pieces):
        base = top if lift is None else top + lift
        weight = jnp.exp2((score - jnp.concatenate([base] * len(lanes), 1)) * SCALE).astype(jnp.bfloat16)
        both = jnp.dot(
            weight, jnp.concatenate([piece[block:], ones], 1), preferred_element_type=jnp.float32
        )
        acc = both[:, :HEAD] if acc is None else acc + both[:, :HEAD]
        total = both[:, HEAD:] if total is None else total + both[:, HEAD:]
    return top, acc, total


def column_copies(place, weight_hbm, into, sems):
    columns = into[0].shape[1]
    copies = []
    for flip, ref in enumerate(into):
        at = pl.ds(pl.multiple_of((place ^ (2 * flip)) * columns, columns), columns)
        copies.append(pltpu.make_async_copy(weight_hbm.at[:, at], ref, sems.at[flip]))
    return copies


def begin_kernel(
    kinds, rank_ref, place_ref, query_hbm, cos_hbm, sin_hbm, weight_hbm, piece_ref,
    rot_ref, top_ref, acc_ref, total_ref, *refs,
):
    away_ref, query_ref, cos_ref, sin_ref, sems, weight_sems = refs
    heads, block, _ = query_ref.shape
    per_span = SPAN // block
    rank, place = rank_ref[0], place_ref[0]
    inner = rank % per_span
    places = [inner, jnp.where(inner == 0, per_span, per_span + 1), per_span + 1][:kinds]
    copies = [pltpu.make_async_copy(query_hbm, query_ref, sems.at[0])]
    for kind, at in enumerate(places):
        rows = pl.ds(pl.multiple_of(at * block, block), block)
        copies.append(pltpu.make_async_copy(cos_hbm.at[rows], cos_ref.at[kind], sems.at[1 + 2 * kind]))
        copies.append(pltpu.make_async_copy(sin_hbm.at[rows], sin_ref.at[kind], sems.at[2 + 2 * kind]))
    for copy in copies:
        copy.start()
    loads = column_copies(place ^ 2, weight_hbm, [away_ref], weight_sems)
    for copy in loads:
        copy.start()
    for copy in copies:
        copy.wait()
    causal = lax.broadcasted_iota(jnp.int32, (block, block), 1) <= lax.broadcasted_iota(
        jnp.int32, (block, block), 0
    )
    def turn(kind):
        for head in range(heads):
            rot_ref[kind, head] = rotated(query_ref[head], cos_ref[kind], sin_ref[kind]).astype(
                jnp.bfloat16
            )

    def blank(kind):
        rot_ref[kind] = jnp.zeros(rot_ref.shape[1:], rot_ref.dtype)

    turn(0)
    for kind in range(1, kinds):
        pl.when(rank >= kind * per_span)(functools.partial(turn, kind))
        pl.when(rank < kind * per_span)(functools.partial(blank, kind))
    later = scores_of([rot_ref[0, 0]], [piece_ref])
    for head in range(heads):
        now = later
        if head + 1 < heads:
            later = scores_of([rot_ref[0, head + 1]], [piece_ref])
        now = [jnp.where(causal, now[0], NEG)]
        top_ref[head], acc_ref[head], total_ref[head] = absorb(now, [None], [piece_ref], None)
    for copy in loads:
        copy.wait()


def begin(kinds, rank, place, queries, tables, out_weight, piece):
    heads, block, _ = queries.shape
    depth = out_weight.shape[0]
    smem, hbm, vmem = (pl.BlockSpec(memory_space=space) for space in (pltpu.SMEM, HBM, VMEM))
    return pl.pallas_call(
        functools.partial(begin_kernel, kinds),
        in_specs=[smem, smem, hbm, hbm, hbm, hbm, vmem],
        out_specs=[vmem] * 5,
        out_shape=[
            jax.ShapeDtypeStruct((kinds, heads, block, HEAD), jnp.bfloat16),
            *[jax.ShapeDtypeStruct((heads, block, HEAD), jnp.float32)] * 3,
            jax.ShapeDtypeStruct((depth, depth), jnp.bfloat16),
        ],
        scratch_shapes=[
            pltpu.VMEM((heads, block, HEAD), jnp.bfloat16),
            pltpu.VMEM((kinds, block, HEAD), jnp.float32),
            pltpu.VMEM((kinds, block, HEAD), jnp.float32),
            pltpu.SemaphoreType.DMA((1 + 2 * kinds,)),
            pltpu.SemaphoreType.DMA((1,)),
        ],
        cost_estimate=LIGHT,
        compiler_params=pltpu.CompilerParams(vmem_limit_bytes=LIMIT),
        name="attend_0",
    )(rank, place, *[in_hbm(x) for x in (queries, *tables, out_weight)], piece)


def attend_kernel(offsets, kinds, first, last, start, rows, stages, rank_ref, rot_ref, *refs):
    pieces, refs = refs[: len(offsets)], refs[len(offsets) :]
    old, refs = ([], refs) if first else (refs[:3], refs[3:])
    loads = []
    if stages:
        place_ref, *refs, sems = refs
        weights, refs, staged = refs[:stages], refs[stages:-stages], refs[-stages:]
        for at, (weight_hbm, ref) in enumerate(zip(weights, staged)):
            loads += column_copies(place_ref[0] ^ 2, weight_hbm, [ref], sems.at[pl.ds(at, 1)])
    for copy in loads:
        copy.start()
    block = pieces[0].shape[0] // 2
    per_span = SPAN // block
    rank = rank_ref[0]
    lifts = [
        jnp.where((rank ^ offset) <= rank, 0.0, -NEG).astype(jnp.float32) if offset else None
        for offset in offsets
    ]
    picked = []
    for offset in offsets:
        kind = min(offset // per_span, 1)
        if kind and kinds > 2:
            back = rank // per_span - (rank ^ offset) // per_span
            kind = jnp.clip(back, 1, kinds - 1)
        picked.append(kind)
    here = slice(start, start + rows)
    if 0 in offsets:
        causal = lax.broadcasted_iota(jnp.int32, (rows, block), 1) <= start + lax.broadcasted_iota(
            jnp.int32, (rows, block), 0
        )

    def scores_at(head):
        scores = scores_of([rot_ref[kind, head, here] for kind in picked], pieces)
        return [
            score if offset else jnp.where(causal, score, NEG)
            for offset, score in zip(offsets, scores)
        ]

    def put(head, top, acc, total):
        if last:
            refs[0][:, head * HEAD : (head + 1) * HEAD] = (acc / total).astype(jnp.bfloat16)
        else:
            refs[0][head], refs[1][head], refs[2][head] = top, acc, total

    def meet():
        later = scores_at(0)
        for head in range(GROUP):
            now = later
            if head + 1 < GROUP:
                later = scores_at(head + 1)
            put(
                head,
                *absorb(now, lifts, pieces, [ref[head, here] for ref in old] or None),
            )

    def keep():
        for head in range(GROUP):
            put(head, *[ref[head, here] for ref in old])

    if first:
        meet()
    else:
        seen = functools.reduce(jnp.logical_or, [(rank ^ offset) <= rank for offset in offsets])
        pl.when(seen)(meet)
        pl.when(jnp.logical_not(seen))(keep)
    for copy in loads:
        copy.wait()


def attend(rank, offsets, rot, pieces, state, last, start, rows, stage=()):
    block = pieces[0].shape[0] // 2
    smem, vmem = (pl.BlockSpec(memory_space=space) for space in (pltpu.SMEM, VMEM))
    if last:
        out_specs = vmem
        out_shape = jax.ShapeDtypeStruct((rows, GROUP * HEAD), jnp.bfloat16)
    else:
        out_specs = [vmem] * 3
        out_shape = [jax.ShapeDtypeStruct((GROUP, rows, HEAD), jnp.float32)] * 3
    args, in_specs, scratch = [], [], []
    if stage:
        place, *weights = stage
        depth = weights[0].shape[0]
        args = [place, *[in_hbm(weight) for weight in weights]]
        in_specs = [smem] + [pl.BlockSpec(memory_space=HBM)] * len(weights)
        out_specs = [*out_specs, *[vmem] * len(weights)]
        out_shape = [
            *out_shape,
            *[jax.ShapeDtypeStruct((depth, depth), jnp.bfloat16)] * len(weights),
        ]
        scratch = [pltpu.SemaphoreType.DMA((len(weights),))]
    return pl.pallas_call(
        functools.partial(
            attend_kernel,
            tuple(offsets),
            rot.shape[0],
            not state,
            last,
            start,
            rows,
            len(stage[1:]),
        ),
        in_specs=[smem] + [vmem] * (1 + len(pieces) + len(state)) + in_specs,
        scratch_shapes=scratch,
        out_specs=out_specs,
        out_shape=out_shape,
        cost_estimate=LIGHT,
        compiler_params=pltpu.CompilerParams(vmem_limit_bytes=LIMIT),
        name="attend_" + "_".join(map(str, offsets)),
    )(rank, rot, *pieces, *state, *args)


def project_kernel(own_ref, twin_ref, own_weight, twin_weight, out_ref):
    out_ref[...] = (
        jnp.dot(own_ref[...], own_weight[...], preferred_element_type=jnp.float32)
        + jnp.dot(twin_ref[...], twin_weight[...], preferred_element_type=jnp.float32)
    ).astype(out_ref.dtype)


def project(own, twin, own_weight, twin_weight, dtype, name):
    vmem = pl.BlockSpec(memory_space=VMEM)
    return pl.pallas_call(
        project_kernel,
        in_specs=[vmem] * 4,
        out_specs=vmem,
        out_shape=jax.ShapeDtypeStruct((own.shape[0], own_weight.shape[1]), dtype),
        cost_estimate=LIGHT,
        compiler_params=pltpu.CompilerParams(vmem_limit_bytes=LIMIT),
        name=name,
    )(own, twin, own_weight, twin_weight)


def home_kernel(count, place_ref, own_hbm, twin_hbm, *refs):
    own_refs, twin_refs, refs = refs[:count], refs[count : 2 * count], refs[2 * count :]
    out_ref, own_weight, twin_weight, sems = refs
    loads = []
    for at, (hbm, ref) in enumerate(((own_hbm, own_weight), (twin_hbm, twin_weight))):
        loads += column_copies(place_ref[0], hbm, [ref], sems.at[pl.ds(at, 1)])
    for load in loads:
        load.start()
    for load in loads:
        load.wait()
    start = 0
    for own, twin in zip(own_refs, twin_refs):
        rows = pl.ds(start, own.shape[0])
        out_ref[rows] = jnp.dot(
            own[...], own_weight[...], preferred_element_type=jnp.float32
        ) + jnp.dot(twin[...], twin_weight[...], preferred_element_type=jnp.float32)
        start += own.shape[0]


def project_home(place, own, twin, own_weight, twin_weight):
    smem, hbm, vmem = (pl.BlockSpec(memory_space=space) for space in (pltpu.SMEM, HBM, VMEM))
    rows = sum(x.shape[0] for x in own)
    depth = own_weight.shape[0]
    return pl.pallas_call(
        functools.partial(home_kernel, len(own)),
        in_specs=[smem, hbm, hbm] + [vmem] * (2 * len(own)),
        out_specs=vmem,
        out_shape=jax.ShapeDtypeStruct((rows, depth), jnp.float32),
        scratch_shapes=[
            pltpu.VMEM((depth, depth), jnp.bfloat16),
            pltpu.VMEM((depth, depth), jnp.bfloat16),
            pltpu.SemaphoreType.DMA((2,)),
        ],
        cost_estimate=LIGHT,
        compiler_params=pltpu.CompilerParams(vmem_limit_bytes=LIMIT),
        name="home",
    )(place, in_hbm(own_weight), in_hbm(twin_weight), *own, *twin)


def close_kernel(start, home_ref, landed_ref, *refs):
    out_hbm, sum_ref, sem = refs[-3:]
    rows = pl.ds(start, sum_ref.shape[0])
    sum_ref[...] = (home_ref[rows] + landed_ref[...].astype(jnp.float32)).astype(sum_ref.dtype)
    copy = pltpu.make_async_copy(sum_ref, out_hbm.at[rows], sem)
    copy.start()
    copy.wait()


def close(start, home, landed, out):
    rows, columns = landed.shape
    vmem, hbm = (pl.BlockSpec(memory_space=space) for space in (VMEM, HBM))
    return pl.pallas_call(
        functools.partial(close_kernel, start),
        in_specs=[vmem, vmem] + ([] if out is None else [hbm]),
        out_specs=hbm,
        out_shape=HBM(home.shape, jnp.bfloat16),
        input_output_aliases={} if out is None else {2: 0},
        scratch_shapes=[pltpu.VMEM((rows, columns), jnp.bfloat16), pltpu.SemaphoreType.DMA],
        cost_estimate=LIGHT,
        compiler_params=pltpu.CompilerParams(vmem_limit_bytes=LIMIT),
        name="close_%d" % start,
    )(home, landed, *([] if out is None else [out]))


def swap(x, axis, size, bits):
    return lax.ppermute(x, axis, [(i, i ^ bits) for i in range(size)])


def swap_late(x, seq, kv, bits):
    pairs = []
    for rank in range(seq):
        for place in range(kv):
            to = (rank ^ bits, place) if 2 * rank >= seq else (rank, place ^ 1)
            pairs.append((rank * kv + place, to[0] * kv + to[1]))
    return lax.ppermute(x, ("seq", "kv"), pairs)


def after(x, *others):
    return lax.optimization_barrier((x, *others))[0]


def make_shards(seq, kv):
    def shards(queries, keys, values, out_weight):
        block = queries.shape[0]
        per_span = SPAN // block
        rank = lax.axis_index("seq").astype(jnp.int32).reshape(1)
        place = lax.axis_index("kv").astype(jnp.int32).reshape(1)
        kinds = min(3, max(2, seq // per_span))
        tables = rope_tables(block)
        by_head = jnp.transpose(queries, (1, 0, 2))
        pieces = {0: prepare(rank, keys[:, 0, :], values[:, 0, :], tables)}

        def send(offset, step, *others):
            pieces[offset] = swap(after(pieces[offset ^ step], *others), "seq", seq, step)

        def pass_on(offset, step, *others):
            source = after(pieces[offset ^ step], *others)
            late = 2 * offset >= seq
            pieces[offset] = swap_late(source, seq, kv, step) if late else swap(source, "seq", seq, step)

        twin_weight = swap(after(out_weight, pieces[0]), "kv", kv, 1)
        for offset in FIRST:
            send(offset, offset)
        rot, *state = begin(
            kinds, rank, place, by_head, tables, out_weight, pieces[0]
        )
        state, staged = state[:3], state[3:]
        for offset in range(2 * per_span, seq, per_span):
            send(offset, offset & -offset)
            for low in range(1, per_span):
                send(offset + low, low)
        calls = CALLS + [list(range(at, at + per_span)) for at in range(2 * per_span, seq, per_span)]

        def blocks(offsets, state, *how):
            return attend(rank, offsets, rot, [pieces[o] for o in offsets], state, *how)

        for offset in LATER:
            pass_on(offset, offset ^ TURN, state[0])
        for offsets, weights in zip(calls[:-1], STAGES + [[]] * len(calls)):
            stage = (place, *[(out_weight, twin_weight)[at] for at in weights]) if weights else ()
            state = blocks(offsets, state, False, 0, block, stage)
            state, staged = state[:3], staged + list(state[3:])
        own, twin, start = [], [], 0
        for rows in ROW_CHUNKS:
            own.append(blocks(calls[-1], state, True, start, rows))
            twin.append(swap(own[-1], "kv", kv, 1))
            start += rows
        landed = []
        for rows in zip(own, twin):
            away = project(
                *rows, *staged, jnp.bfloat16, "away"
            )
            landed.append(swap(away, "kv", kv, 2))
        home = project_home(place, own, twin, out_weight, twin_weight)
        out, start = None, 0
        for rows in landed:
            out = close(start, home, rows, out)
            start += rows.shape[0]
        return out

    return shards


def solution(mesh):
    return jax.shard_map(
        make_shards(mesh.shape["seq"], mesh.shape["kv"]),
        mesh=mesh,
        in_specs=(P("seq", "kv", None), P("seq", "kv", None), P("seq", "kv", None), P("kv", None)),
        out_specs=P("seq", "kv"),
        check_vma=False,
    )
```

```python
import functools
import math

import jax
import jax.numpy as jnp
import numpy as np
from jax import lax
from jax.experimental import pallas as pl
from jax.experimental.pallas import tpu as pltpu
from jax.sharding import PartitionSpec as P

HEAD = 128
GROUP = 7
SPAN = 1024
LOCAL = 32
THETA = 10000000.0
NEG = -1e30
SCALE = math.log2(math.e) / math.sqrt(HEAD)
ROW_CHUNKS = (128, 128)
TURN = 6
FIRST = [6, 1, 2]
CALLS = [[1, 2], [3, 6], [5], [4, 7]]
LATER = [5, 4, 7]
STAGES = [[], [1]]
VMEM = pltpu.MemorySpace.VMEM
HBM = pltpu.MemorySpace.HBM
LIMIT = 24 * 2**20
LIGHT = pl.CostEstimate(flops=1, bytes_accessed=1, transcendentals=0)


def rope_tables(block):
    inverse = np.exp(np.arange(HEAD // 2, dtype=np.float64) * (-2.0 * math.log(THETA) / HEAD))
    inner = np.arange(SPAN)
    first = np.minimum(np.arange(block) + SPAN, SPAN + LOCAL)
    far = np.full((block,), SPAN + LOCAL)
    angles = np.concatenate([inner, first, far])[:, None] * inverse
    cosine, sine = np.cos(angles), np.sin(angles)
    return (
        jnp.asarray(np.concatenate([cosine, cosine], 1), jnp.float32),
        jnp.asarray(np.concatenate([-sine, sine], 1), jnp.float32),
    )


def rotated(x, cosine, sine):
    x = x.astype(jnp.float32)
    return x * cosine + pltpu.roll(x, HEAD // 2, 1) * sine


def in_hbm(x):
    return pltpu.with_memory_space_constraint(x, HBM)


def prepare_kernel(rank_ref, key_hbm, value_hbm, cos_hbm, sin_hbm, out_ref, key_ref, cos_ref, sin_ref, sems):
    block = key_ref.shape[0]
    rows = pl.ds(pl.multiple_of(rank_ref[0] % (SPAN // block) * block, block), block)
    copies = [
        pltpu.make_async_copy(key_hbm, key_ref, sems.at[0]),
        pltpu.make_async_copy(cos_hbm.at[rows], cos_ref, sems.at[1]),
        pltpu.make_async_copy(sin_hbm.at[rows], sin_ref, sems.at[2]),
        pltpu.make_async_copy(value_hbm, out_ref.at[pl.ds(block, block)], sems.at[3]),
    ]
    for copy in copies:
        copy.start()
    for copy in copies:
        copy.wait()
    out_ref[:block] = rotated(key_ref[...], cos_ref[...], sin_ref[...]).astype(jnp.bfloat16)


def prepare(rank, keys, values, tables):
    block = keys.shape[0]
    return pl.pallas_call(
        prepare_kernel,
        in_specs=[pl.BlockSpec(memory_space=pltpu.SMEM)] + [pl.BlockSpec(memory_space=HBM)] * 4,
        out_specs=pl.BlockSpec(memory_space=VMEM),
        out_shape=jax.ShapeDtypeStruct((2 * block, HEAD), jnp.bfloat16),
        scratch_shapes=[
            pltpu.VMEM((block, HEAD), jnp.bfloat16),
            pltpu.VMEM((block, HEAD), jnp.float32),
            pltpu.VMEM((block, HEAD), jnp.float32),
            pltpu.SemaphoreType.DMA((4,)),
        ],
        compiler_params=pltpu.CompilerParams(vmem_limit_bytes=LIMIT),
        name="rotate_keys",
    )(rank, *[in_hbm(x) for x in (keys, values, *tables)])


def scores_of(query, pieces):
    block = pieces[0].shape[0] // 2
    return [
        lax.dot_general(
            q, piece[:block], (((1,), (1,)), ((), ())), preferred_element_type=jnp.float32
        )
        for q, piece in zip(query, pieces)
    ]


def absorb(scores, lifts, pieces, old):
    block = pieces[0].shape[0] // 2
    lanes = [slice(at, at + HEAD) for at in range(0, block, HEAD)]
    peak = None
    for score, lift in zip(scores, lifts):
        high = functools.reduce(jnp.maximum, [score[:, lane] for lane in lanes])
        if lift is not None:
            high = high - lift
        peak = high if peak is None else jnp.maximum(peak, high)
    top = jnp.max(peak, axis=1, keepdims=True)
    if old is None:
        top = jnp.broadcast_to(top, peak.shape)
        acc, total = None, None
    else:
        top = jnp.maximum(top, old[0])
        factor = jnp.exp2((old[0] - top) * SCALE)
        acc, total = factor * old[1], factor * old[2]
    ones = jnp.ones((block, HEAD), jnp.bfloat16)
    for score, lift, piece in zip(scores, lifts, pieces):
        base = top if lift is None else top + lift
        weight = jnp.exp2((score - jnp.concatenate([base] * len(lanes), 1)) * SCALE).astype(jnp.bfloat16)
        both = jnp.dot(
            weight, jnp.concatenate([piece[block:], ones], 1), preferred_element_type=jnp.float32
        )
        acc = both[:, :HEAD] if acc is None else acc + both[:, :HEAD]
        total = both[:, HEAD:] if total is None else total + both[:, HEAD:]
    return top, acc, total


def column_copies(place, weight_hbm, into, sems):
    columns = into[0].shape[1]
    copies = []
    for flip, ref in enumerate(into):
        at = pl.ds(pl.multiple_of((place ^ (2 * flip)) * columns, columns), columns)
        copies.append(pltpu.make_async_copy(weight_hbm.at[:, at], ref, sems.at[flip]))
    return copies


def begin_kernel(
    kinds, rank_ref, place_ref, query_hbm, cos_hbm, sin_hbm, weight_hbm, piece_ref,
    rot_ref, top_ref, acc_ref, total_ref, *refs,
):
    away_ref, query_ref, cos_ref, sin_ref, sems, weight_sems = refs
    heads, block, _ = query_ref.shape
    per_span = SPAN // block
    rank, place = rank_ref[0], place_ref[0]
    inner = rank % per_span
    places = [inner, jnp.where(inner == 0, per_span, per_span + 1), per_span + 1][:kinds]
    copies = [pltpu.make_async_copy(query_hbm, query_ref, sems.at[0])]
    for kind, at in enumerate(places):
        rows = pl.ds(pl.multiple_of(at * block, block), block)
        copies.append(pltpu.make_async_copy(cos_hbm.at[rows], cos_ref.at[kind], sems.at[1 + 2 * kind]))
        copies.append(pltpu.make_async_copy(sin_hbm.at[rows], sin_ref.at[kind], sems.at[2 + 2 * kind]))
    for copy in copies:
        copy.start()
    loads = column_copies(place ^ 2, weight_hbm, [away_ref], weight_sems)
    for copy in loads:
        copy.start()
    for copy in copies:
        copy.wait()
    causal = lax.broadcasted_iota(jnp.int32, (block, block), 1) <= lax.broadcasted_iota(
        jnp.int32, (block, block), 0
    )
    def turn(kind):
        for head in range(heads):
            rot_ref[kind, head] = rotated(query_ref[head], cos_ref[kind], sin_ref[kind]).astype(
                jnp.bfloat16
            )

    def blank(kind):
        rot_ref[kind] = jnp.zeros(rot_ref.shape[1:], rot_ref.dtype)

    turn(0)
    for kind in range(1, kinds):
        pl.when(rank >= kind * per_span)(functools.partial(turn, kind))
        pl.when(rank < kind * per_span)(functools.partial(blank, kind))
    later = scores_of([rot_ref[0, 0]], [piece_ref])
    for head in range(heads):
        now = later
        if head + 1 < heads:
            later = scores_of([rot_ref[0, head + 1]], [piece_ref])
        now = [jnp.where(causal, now[0], NEG)]
        top_ref[head], acc_ref[head], total_ref[head] = absorb(now, [None], [piece_ref], None)
    for copy in loads:
        copy.wait()


def begin(kinds, rank, place, queries, tables, out_weight, piece):
    heads, block, _ = queries.shape
    depth = out_weight.shape[0]
    smem, hbm, vmem = (pl.BlockSpec(memory_space=space) for space in (pltpu.SMEM, HBM, VMEM))
    return pl.pallas_call(
        functools.partial(begin_kernel, kinds),
        in_specs=[smem, smem, hbm, hbm, hbm, hbm, vmem],
        out_specs=[vmem] * 5,
        out_shape=[
            jax.ShapeDtypeStruct((kinds, heads, block, HEAD), jnp.bfloat16),
            *[jax.ShapeDtypeStruct((heads, block, HEAD), jnp.float32)] * 3,
            jax.ShapeDtypeStruct((depth, depth), jnp.bfloat16),
        ],
        scratch_shapes=[
            pltpu.VMEM((heads, block, HEAD), jnp.bfloat16),
            pltpu.VMEM((kinds, block, HEAD), jnp.float32),
            pltpu.VMEM((kinds, block, HEAD), jnp.float32),
            pltpu.SemaphoreType.DMA((1 + 2 * kinds,)),
            pltpu.SemaphoreType.DMA((1,)),
        ],
        cost_estimate=LIGHT,
        compiler_params=pltpu.CompilerParams(vmem_limit_bytes=LIMIT),
        name="attend_0",
    )(rank, place, *[in_hbm(x) for x in (queries, *tables, out_weight)], piece)


def attend_kernel(offsets, kinds, first, last, start, rows, stages, rank_ref, rot_ref, *refs):
    pieces, refs = refs[: len(offsets)], refs[len(offsets) :]
    old, refs = ([], refs) if first else (refs[:3], refs[3:])
    loads = []
    if stages:
        place_ref, *refs, sems = refs
        weights, refs, staged = refs[:stages], refs[stages:-stages], refs[-stages:]
        for at, (weight_hbm, ref) in enumerate(zip(weights, staged)):
            loads += column_copies(place_ref[0] ^ 2, weight_hbm, [ref], sems.at[pl.ds(at, 1)])
    for copy in loads:
        copy.start()
    block = pieces[0].shape[0] // 2
    per_span = SPAN // block
    rank = rank_ref[0]
    lifts = [
        jnp.where((rank ^ offset) <= rank, 0.0, -NEG).astype(jnp.float32) if offset else None
        for offset in offsets
    ]
    picked = []
    for offset in offsets:
        kind = min(offset // per_span, 1)
        if kind and kinds > 2:
            back = rank // per_span - (rank ^ offset) // per_span
            kind = jnp.clip(back, 1, kinds - 1)
        picked.append(kind)
    here = slice(start, start + rows)
    if 0 in offsets:
        causal = lax.broadcasted_iota(jnp.int32, (rows, block), 1) <= start + lax.broadcasted_iota(
            jnp.int32, (rows, block), 0
        )

    def scores_at(head):
        scores = scores_of([rot_ref[kind, head, here] for kind in picked], pieces)
        return [
            score if offset else jnp.where(causal, score, NEG)
            for offset, score in zip(offsets, scores)
        ]

    def put(head, top, acc, total):
        if last:
            refs[0][:, head * HEAD : (head + 1) * HEAD] = (acc / total).astype(jnp.bfloat16)
        else:
            refs[0][head], refs[1][head], refs[2][head] = top, acc, total

    def meet():
        later = scores_at(0)
        for head in range(GROUP):
            now = later
            if head + 1 < GROUP:
                later = scores_at(head + 1)
            put(
                head,
                *absorb(now, lifts, pieces, [ref[head, here] for ref in old] or None),
            )

    def keep():
        for head in range(GROUP):
            put(head, *[ref[head, here] for ref in old])

    if first:
        meet()
    else:
        seen = functools.reduce(jnp.logical_or, [(rank ^ offset) <= rank for offset in offsets])
        pl.when(seen)(meet)
        pl.when(jnp.logical_not(seen))(keep)
    for copy in loads:
        copy.wait()


def attend(rank, offsets, rot, pieces, state, last, start, rows, stage=()):
    block = pieces[0].shape[0] // 2
    smem, vmem = (pl.BlockSpec(memory_space=space) for space in (pltpu.SMEM, VMEM))
    if last:
        out_specs = vmem
        out_shape = jax.ShapeDtypeStruct((rows, GROUP * HEAD), jnp.bfloat16)
    else:
        out_specs = [vmem] * 3
        out_shape = [jax.ShapeDtypeStruct((GROUP, rows, HEAD), jnp.float32)] * 3
    args, in_specs, scratch = [], [], []
    if stage:
        place, *weights = stage
        depth = weights[0].shape[0]
        args = [place, *[in_hbm(weight) for weight in weights]]
        in_specs = [smem] + [pl.BlockSpec(memory_space=HBM)] * len(weights)
        out_specs = [*out_specs, *[vmem] * len(weights)]
        out_shape = [
            *out_shape,
            *[jax.ShapeDtypeStruct((depth, depth), jnp.bfloat16)] * len(weights),
        ]
        scratch = [pltpu.SemaphoreType.DMA((len(weights),))]
    return pl.pallas_call(
        functools.partial(
            attend_kernel,
            tuple(offsets),
            rot.shape[0],
            not state,
            last,
            start,
            rows,
            len(stage[1:]),
        ),
        in_specs=[smem] + [vmem] * (1 + len(pieces) + len(state)) + in_specs,
        scratch_shapes=scratch,
        out_specs=out_specs,
        out_shape=out_shape,
        cost_estimate=LIGHT,
        compiler_params=pltpu.CompilerParams(vmem_limit_bytes=LIMIT),
        name="attend_" + "_".join(map(str, offsets)),
    )(rank, rot, *pieces, *state, *args)


def project_kernel(own_ref, twin_ref, own_weight, twin_weight, out_ref):
    out_ref[...] = (
        jnp.dot(own_ref[...], own_weight[...], preferred_element_type=jnp.float32)
        + jnp.dot(twin_ref[...], twin_weight[...], preferred_element_type=jnp.float32)
    ).astype(out_ref.dtype)


def project(own, twin, own_weight, twin_weight, dtype, name):
    vmem = pl.BlockSpec(memory_space=VMEM)
    return pl.pallas_call(
        project_kernel,
        in_specs=[vmem] * 4,
        out_specs=vmem,
        out_shape=jax.ShapeDtypeStruct((own.shape[0], own_weight.shape[1]), dtype),
        cost_estimate=LIGHT,
        compiler_params=pltpu.CompilerParams(vmem_limit_bytes=LIMIT),
        name=name,
    )(own, twin, own_weight, twin_weight)


def home_kernel(count, place_ref, own_hbm, twin_hbm, *refs):
    own_refs, twin_refs, refs = refs[:count], refs[count : 2 * count], refs[2 * count :]
    out_ref, own_weight, twin_weight, sems = refs
    loads = []
    for at, (hbm, ref) in enumerate(((own_hbm, own_weight), (twin_hbm, twin_weight))):
        loads += column_copies(place_ref[0], hbm, [ref], sems.at[pl.ds(at, 1)])
    for load in loads:
        load.start()
    for load in loads:
        load.wait()
    start = 0
    for own, twin in zip(own_refs, twin_refs):
        rows = pl.ds(start, own.shape[0])
        out_ref[rows] = jnp.dot(
            own[...], own_weight[...], preferred_element_type=jnp.float32
        ) + jnp.dot(twin[...], twin_weight[...], preferred_element_type=jnp.float32)
        start += own.shape[0]


def project_home(place, own, twin, own_weight, twin_weight):
    smem, hbm, vmem = (pl.BlockSpec(memory_space=space) for space in (pltpu.SMEM, HBM, VMEM))
    rows = sum(x.shape[0] for x in own)
    depth = own_weight.shape[0]
    return pl.pallas_call(
        functools.partial(home_kernel, len(own)),
        in_specs=[smem, hbm, hbm] + [vmem] * (2 * len(own)),
        out_specs=vmem,
        out_shape=jax.ShapeDtypeStruct((rows, depth), jnp.float32),
        scratch_shapes=[
            pltpu.VMEM((depth, depth), jnp.bfloat16),
            pltpu.VMEM((depth, depth), jnp.bfloat16),
            pltpu.SemaphoreType.DMA((2,)),
        ],
        cost_estimate=LIGHT,
        compiler_params=pltpu.CompilerParams(vmem_limit_bytes=LIMIT),
        name="home",
    )(place, in_hbm(own_weight), in_hbm(twin_weight), *own, *twin)


def close_kernel(start, home_ref, landed_ref, *refs):
    out_hbm, sum_ref, sem = refs[-3:]
    rows = pl.ds(start, sum_ref.shape[0])
    sum_ref[...] = (home_ref[rows] + landed_ref[...].astype(jnp.float32)).astype(sum_ref.dtype)
    copy = pltpu.make_async_copy(sum_ref, out_hbm.at[rows], sem)
    copy.start()
    copy.wait()


def close(start, home, landed, out):
    rows, columns = landed.shape
    vmem, hbm = (pl.BlockSpec(memory_space=space) for space in (VMEM, HBM))
    return pl.pallas_call(
        functools.partial(close_kernel, start),
        in_specs=[vmem, vmem] + ([] if out is None else [hbm]),
        out_specs=hbm,
        out_shape=HBM(home.shape, jnp.bfloat16),
        input_output_aliases={} if out is None else {2: 0},
        scratch_shapes=[pltpu.VMEM((rows, columns), jnp.bfloat16), pltpu.SemaphoreType.DMA],
        cost_estimate=LIGHT,
        compiler_params=pltpu.CompilerParams(vmem_limit_bytes=LIMIT),
        name="close_%d" % start,
    )(home, landed, *([] if out is None else [out]))


def swap(x, axis, size, bits):
    return lax.ppermute(x, axis, [(i, i ^ bits) for i in range(size)])


def swap_late(x, seq, kv, bits):
    pairs = []
    for rank in range(seq):
        for place in range(kv):
            to = (rank ^ bits, place) if 2 * rank >= seq else (rank, place ^ 1)
            pairs.append((rank * kv + place, to[0] * kv + to[1]))
    return lax.ppermute(x, ("seq", "kv"), pairs)


def after(x, *others):
    return lax.optimization_barrier((x, *others))[0]


def make_shards(seq, kv):
    def shards(queries, keys, values, out_weight):
        block = queries.shape[0]
        per_span = SPAN // block
        rank = lax.axis_index("seq").astype(jnp.int32).reshape(1)
        place = lax.axis_index("kv").astype(jnp.int32).reshape(1)
        kinds = min(3, max(2, seq // per_span))
        tables = rope_tables(block)
        by_head = jnp.transpose(queries, (1, 0, 2))
        pieces = {0: prepare(rank, keys[:, 0, :], values[:, 0, :], tables)}

        def send(offset, step, *others):
            pieces[offset] = swap(after(pieces[offset ^ step], *others), "seq", seq, step)

        def pass_on(offset, step, *others):
            source = after(pieces[offset ^ step], *others)
            late = 2 * offset >= seq
            pieces[offset] = swap_late(source, seq, kv, step) if late else swap(source, "seq", seq, step)

        twin_weight = swap(after(out_weight, pieces[0]), "kv", kv, 1)
        for offset in FIRST:
            send(offset, offset)
        rot, *state = begin(
            kinds, rank, place, by_head, tables, out_weight, pieces[0]
        )
        state, staged = state[:3], state[3:]
        send(3, 3, state[0])
        for offset in range(2 * per_span, seq, per_span):
            send(offset, offset & -offset)
            for low in range(1, per_span):
                send(offset + low, low)
        calls = CALLS + [list(range(at, at + per_span)) for at in range(2 * per_span, seq, per_span)]

        def blocks(offsets, state, *how):
            return attend(rank, offsets, rot, [pieces[o] for o in offsets], state, *how)

        for offset in LATER:
            pass_on(offset, offset ^ TURN, state[0])
        for offsets, weights in zip(calls[:-1], STAGES + [[]] * len(calls)):
            stage = (place, *[(out_weight, twin_weight)[at] for at in weights]) if weights else ()
            state = blocks(offsets, state, False, 0, block, stage)
            state, staged = state[:3], staged + list(state[3:])
        own, twin, start = [], [], 0
        for rows in ROW_CHUNKS:
            own.append(blocks(calls[-1], state, True, start, rows))
            twin.append(swap(own[-1], "kv", kv, 1))
            start += rows
        landed = []
        for rows in zip(own, twin):
            away = project(
                *rows, *staged, jnp.bfloat16, "away"
            )
            landed.append(swap(away, "kv", kv, 2))
        home = project_home(place, own, twin, out_weight, twin_weight)
        out, start = None, 0
        for rows in landed:
            out = close(start, home, rows, out)
            start += rows.shape[0]
        return out

    return shards


def solution(mesh):
    return jax.shard_map(
        make_shards(mesh.shape["seq"], mesh.shape["kv"]),
        mesh=mesh,
        in_specs=(P("seq", "kv", None), P("seq", "kv", None), P("seq", "kv", None), P("kv", None)),
        out_specs=P("seq", "kv"),
        check_vma=False,
    )
```
